128 devices in a mesh: rows: 64 (over z, x_lo, y, core), cols: 2 (over x_hi).
Axes of the slice: x: 4 (x_hi: 2, x_lo: 2; x = x_hi * 2 + x_lo), y: 4, z: 4, core: 2. Of those that a mesh axis runs over, the one named last changes fastest.
Arguments:
- blocks: bfloat16 [81920, 128, 128], P(('rows', 'cols')), may hold values from -0.1875 to 0.1875
- block_row: int32 [81920], P(('rows', 'cols')), may hold values from 0 to 159
- block_col: int32 [81920], P(('rows', 'cols')), may hold values from 0 to 1023
- right_sides: float32 [10240, 8, 128], P('rows'), as said below
- precond: float32 [2048, 128, 128], P(('cols', 'rows')), as said below
Outputs:
- solution: float32 [2048, 8, 128], P(('cols', 'rows'))
- left_vector: float32 [10240, 8, 128], P('rows')
The draws below stay inside these ranges and needn't reach their ends.
Inputs may be any that keep to these rules, and one draw needn't show every extreme that they name: `block_row`: each stored block's row position within its row shard. `block_col`: each stored block's column position within its column shard; positions may repeat. `right_sides`: rows of each right-hand side block have positive scales that differ from block to block. `precond`: each block is upper triangular with a positive diagonal.
All inputs are finite; a program needn't handle non-finite values.
Results may differ from the reference program's by a relative error of at most 0.025.
Values may be sent and summed in bfloat16 or wider, within the bound.
No kernel may reach another device: no remote copies, remote signals or barrier semaphores. Data moves between devices by JAX's collectives and lax.ppermute only.
A program may use at most 128 MiB of HBM per device.

```python
import math
import jax
import jax.numpy as jnp
from jax import lax

BLK = 128
RHS = 8
RB_DEV = 160
BPR = 4
COLS_DEV = 16
ITERS = 3
NB_DEV = 640
NBLK = 81920
NROWBLK = 10240
NCOLBLK = 2048
N_ROWS = 64
N_COLS = 2


def draw_right_sides(key, part):
    key = jax.random.fold_in(key, 7)
    first, second = jax.random.split(key, 2)
    scales = jnp.exp(jax.random.uniform(first, (NROWBLK, 1, 1), jnp.float32, 0.0, math.log(10.0)))
    base = jax.random.normal(second, (NROWBLK, RHS, BLK), jnp.float32)
    return base * scales


def draw_precond(key, part):
    key = jax.random.fold_in(key, 5)
    first, second = jax.random.split(key, 2)
    upper = (jnp.arange(BLK)[:, None] < jnp.arange(BLK)[None, :]).astype(jnp.float32)
    eye_part = (jnp.arange(BLK)[:, None] == jnp.arange(BLK)[None, :]).astype(jnp.float32)
    off = jax.random.normal(first, (NCOLBLK, BLK, BLK), jnp.float32) * (0.6 / BLK ** 0.5)
    diag = jax.random.uniform(second, (NCOLBLK, 1, BLK), jnp.float32, 0.5, 1.5)
    return off * upper[None] + diag * eye_part[None]


def set_ends(array, key, least, high):
    longest = array.shape.index(max(array.shape))
    spots = []
    for shift in (0, 1):
        where = [jax.random.randint(jax.random.fold_in(key, axis), (), 0, length) for axis, length in enumerate(array.shape)]
        where[longest] = (where[longest] + shift) % array.shape[longest]
        spots.append(tuple(where))
    return array.at[spots[0]].set(least).at[spots[1]].set(high)


def block_levels(own_key, shape, shards, least, high):
    factor_of, own = 1.0, jax.random.fold_in(own_key, 6)
    for position, shards_of in shards:
        steps = jnp.exp(jax.random.uniform(jax.random.fold_in(own, position), (shards_of,), jnp.float32, least / len(shards), high / len(shards)))
        factor_of = factor_of * jnp.repeat(steps, shape[position] // shards_of).reshape([-1 if axis == position else 1 for axis in range(len(shape))])
    return factor_of


def noise(own_key, extent, spread, limit, cuts=(), held_as=jnp.bfloat16):
    entries = jax.random.normal(own_key, extent, jnp.float32) * spread
    if len(cuts) > 0:
        entries = block_levels(own_key, extent, cuts, -0.22, 0.18) * entries
    return jnp.clip(entries, min=-limit, max=limit).astype(held_as)


def setup_inputs(seed: int = 0) -> dict:
    key_list = jax.random.split(jax.random.key(seed), 6)
    return {
        "blocks": noise(key_list[0], (NBLK, BLK, BLK), (BLK * BPR * N_COLS) ** -0.5, 0.1875, ((0, 128),)),
        "block_row": set_ends(jax.random.randint(key_list[1], (NBLK,), 0, RB_DEV), jax.random.fold_in(key_list[1], 1), 0, RB_DEV - 1).astype(jnp.int32),
        "block_col": set_ends(jax.random.randint(key_list[2], (NBLK,), 0, COLS_DEV * N_ROWS), jax.random.fold_in(key_list[2], 1), 0, (COLS_DEV * N_ROWS) - 1).astype(jnp.int32),
        "right_sides": draw_right_sides(jax.random.fold_in(key_list[5], 71), 0),
        "precond": draw_precond(jax.random.fold_in(key_list[5], 71), 0),
    }


EPS = 1e-06

def widen(vector):
    return vector[None, :, None]

def norm_of(field):
    return jnp.sqrt(lax.optimization_barrier(jnp.sum(field * field, axis=(0, 2))) + EPS)

def reference(blocks, block_row, block_col, right_sides, precond):
    span = COLS_DEV * N_ROWS
    groups = NBLK // NB_DEV
    device_ids = jnp.arange(NBLK, dtype=jnp.int32) // NB_DEV
    glob_rows = (device_ids // N_COLS * RB_DEV + block_row).astype(jnp.int32)
    glob_cols = (device_ids % N_COLS * span + block_col).astype(jnp.int32)
    grouped = blocks.reshape(groups, NB_DEV, BLK, BLK)
    rows_grouped = glob_rows.reshape(groups, NB_DEV)
    cols_grouped = glob_cols.reshape(groups, NB_DEV)

    def forward(scaled):

        def add_group(accum, piece):
            mats, rows_idx, cols_idx = piece
            picked = scaled[cols_idx].astype(jnp.float32)
            prod = jnp.einsum('nkb,ncb->nkc', picked, mats.astype(jnp.float32))
            return (accum.at[rows_idx].add(prod), None)
        start = jnp.zeros((NROWBLK, RHS, BLK), jnp.float32)
        return lax.scan(add_group, start, (grouped, rows_grouped, cols_grouped))[0]

    def backward(left):
        narrow = left.astype(jnp.bfloat16)

        def add_group(accum, piece):
            mats, rows_idx, cols_idx = piece
            picked = narrow[rows_idx].astype(jnp.float32)
            prod = jnp.einsum('nkc,ncb->nkb', picked, mats.astype(jnp.float32))
            return (accum.at[cols_idx].add(prod), None)
        start = jnp.zeros((NCOLBLK, RHS, BLK), jnp.float32)
        return lax.scan(add_group, start, (grouped, rows_grouped, cols_grouped))[0]

    def apply_pre(field):
        return jnp.einsum('ckb,cbd->ckd', field, precond, precision=lax.Precision.HIGHEST)

    def apply_pre_t(field):
        return jnp.einsum('ckd,cbd->ckb', field, precond, precision=lax.Precision.HIGHEST)
    beta_norm = norm_of(right_sides)
    left_vector = right_sides / widen(beta_norm)
    col_term = apply_pre_t(backward(left_vector))
    phibar = beta_norm
    iterate = jnp.zeros((NCOLBLK, RHS, BLK), jnp.float32)
    search = iterate
    rhobar = beta_norm
    right = iterate
    for sweep in range(ITERS + 1):
        alpha_norm = norm_of(col_term)
        fresh = col_term / widen(alpha_norm)
        if sweep == 0:
            search = fresh
            rhobar = alpha_norm
        else:
            rotation = jnp.sqrt(rhobar * rhobar + beta_norm * beta_norm)
            cosine = rhobar / rotation
            sine_part = beta_norm / rotation
            theta_term = sine_part * alpha_norm
            rhobar = -cosine * alpha_norm
            phi_term = cosine * phibar
            phibar = sine_part * phibar
            iterate = iterate + widen(phi_term / rotation) * search
            search = fresh - widen(theta_term / rotation) * search
        right = fresh
        if sweep < ITERS:
            scaled = apply_pre(col_term).astype(jnp.bfloat16)
            product = forward(scaled)
            row_term = product / widen(alpha_norm) - widen(alpha_norm) * left_vector
            beta_norm = norm_of(row_term)
            left_vector = row_term / widen(beta_norm)
            col_term = apply_pre_t(backward(left_vector)) - widen(beta_norm) * right
    return (apply_pre(iterate), left_vector)
```

```python
import functools

import jax
import jax.numpy as jnp
from jax import lax
from jax.experimental import pallas as pl
from jax.experimental.pallas import tpu as pltpu
from jax.sharding import PartitionSpec as P

ITERS = 3


EPS = 1e-06
HIGHEST = lax.Precision.HIGHEST
F32 = jnp.float32
BF16 = jnp.bfloat16
VM = pl.BlockSpec(memory_space=pltpu.VMEM)
SM = pl.BlockSpec(memory_space=pltpu.SMEM)
LATE = 16


def params():
    return pltpu.CompilerParams(vmem_limit_bytes=32 << 20)


def like(shape, dtype=F32):
    return jax.ShapeDtypeStruct(shape, dtype)


def pack(total, first):
    half = total * 0.5
    top = half.astype(BF16).astype(F32)
    middle = (half - top).astype(BF16).astype(F32)
    low = half - top - middle
    lane = lax.broadcasted_iota(jnp.int32, (total.shape[0], 128), 1) - first
    terms = jnp.where(lane == 0, top, jnp.where(lane == 1, middle, jnp.where(lane == 2, low, 0.0)))
    return terms.astype(BF16)


def unpack(block):
    return jnp.sum(block, axis=-1, keepdims=True) * 2.0


def squares(field):
    return jnp.sum(jnp.sum(field * field, axis=0), axis=-1, keepdims=True)


def accumulate(products, source, target, table, blocks, total):
    count = blocks.shape[0]
    unroll = next(u for u in (128, 64, 32, 16, 8, 4, 2) if count % u == 0)

    def add(base, pending):
        at, term = pending
        spot = target[base + at]
        total[spot] = total[spot] + term

    def step(i, carry):
        base = i * unroll
        pending = []
        for u in range(0, unroll, 2):
            pair = jnp.concatenate([table[source[base + u]], table[source[base + u + 1]]], axis=0)
            pending += list(zip((u, u + 1), products(pair, blocks[pl.ds(base + u, 2)])))
            while len(pending) > LATE:
                add(base, pending.pop(0))
        for item in pending:
            add(base, item)
        return carry

    lax.fori_loop(0, count // unroll, step, 0)


def forward_pair(pair, blocks):
    both = lax.dot_general(
        pair.astype(BF16),
        blocks.reshape(-1, blocks.shape[2]),
        (((1,), (1,)), ((), ())),
        preferred_element_type=F32,
    )
    size = blocks.shape[1]
    half = pair.shape[0] // 2
    return both[:half, :size], both[half:, size:]


def backward_pair(pair, blocks):
    half = pair.shape[0] // 2
    none = jnp.zeros((half, pair.shape[1]), F32)
    spread = jnp.concatenate(
        [jnp.concatenate([pair[:half], none], axis=1), jnp.concatenate([none, pair[half:]], axis=1)], axis=0
    )
    both = jnp.dot(spread.astype(BF16), blocks.reshape(-1, blocks.shape[2]), preferred_element_type=F32)
    return both[:half], both[half:]


def send_sums(here, row_term, row, spot, blocks, kept, sent, total):
    total[...] = jnp.zeros_like(total)
    accumulate(backward_pair, row, spot, row_term, blocks, total)
    half = kept.shape[0] * kept.shape[1]
    kept[...] = total[:half].astype(BF16).reshape(kept.shape)
    sent[...] = total[half:].astype(BF16).reshape(sent.shape)
    norm = pack(squares(row_term[...]), 3 * here[0])
    last = kept.shape[1] - 1
    for chip in range(kept.shape[0]):
        kept[chip, last] = norm
        sent[chip, last] = norm


def first_kernel(here, row, spot, right_sides, blocks, kept, sent, total):
    send_sums(here, right_sides, row, spot, blocks, kept, sent, total)


def new_row_term(mine, other, before, beta, row_term, alpha):
    count = before.shape[0]
    norm = jnp.sqrt(unpack(mine[count].astype(F32)) + unpack(other[count].astype(F32)) + EPS)
    alpha[...] = jnp.broadcast_to(norm, alpha.shape)
    product = mine[:count].astype(F32) + other[:count].astype(F32)
    row_term[...] = product * (1.0 / alpha[...])[None] - before[...] * (alpha[...] / beta[...])[None]


def back_kernel(here, row, spot, mine, other, before, beta, blocks, row_term, alpha, kept, sent, total):
    new_row_term(mine, other, before, beta, row_term, alpha)
    send_sums(here, row_term, row, spot, blocks, kept, sent, total)


def finish_kernel(mine, other, before, beta, row_term, alpha, norms):
    new_row_term(mine, other, before, beta, row_term, alpha)
    norms[...] = jnp.broadcast_to(squares(row_term[...])[None], norms.shape)


def forward_kernel(step, row, spot, mine, other, blocks, product, table, total):
    half = mine.shape[0]
    table[:half] = mine[...].astype(F32)
    table[half:] = other[...].astype(F32)
    total[...] = jnp.zeros_like(total)
    accumulate(forward_pair, spot, row, table, blocks, total)
    count = total.shape[0]
    product[:count] = total[...].astype(BF16)
    norm = jnp.zeros(total.shape[1:], F32)
    for last in range(step - 1, half, step):
        norm = norm + table[last] + table[half + last]
    product[count] = pack(unpack(norm), 0)


def advance(state, alpha, beta):
    col_term, search, iterate, rhobar, phibar = state
    fresh = col_term / alpha
    rotation = jnp.sqrt(rhobar * rhobar + beta * beta)
    cosine = rhobar / rotation
    sine = beta / rotation
    theta = sine * alpha
    phi = cosine * phibar
    iterate = iterate + (phi / rotation) * search
    search = fresh - (theta / rotation) * search
    return fresh, search, iterate, -cosine * alpha, sine * phibar


def column_kernel(sweep, chunks, precond, *refs):
    if sweep == 0:
        col_term, beta, scaled = refs
    elif sweep == 1:
        before, alpha, beta_before, col_term, beta, scaled, search, iterate, rhobar, phibar = refs
        fresh = before[...] / alpha[...][None]
        search[...] = fresh
        iterate[...] = jnp.zeros_like(iterate)
        rhobar[...] = alpha[...]
        phibar[...] = beta_before[...]
    else:
        (before, alpha, beta_before, search_in, iterate_in, rhobar_in, phibar_in) = refs[:7]
        col_term, beta, scaled, search, iterate, rhobar, phibar = refs[7:]
        state = (before[...], search_in[...], iterate_in[...], rhobar_in[...], phibar_in[...])
        fresh, search[...], iterate[...], rhobar[...], phibar[...] = advance(state, alpha[...], beta_before[...])
    own = col_term.shape[0]
    gathered = jnp.sum(chunks[...].astype(F32), axis=0)
    beta[...] = jnp.broadcast_to(jnp.sqrt(unpack(gathered[own]) + EPS), beta.shape)
    gathered = gathered * (1.0 / beta[...])[None]
    norm = jnp.zeros(beta.shape, F32)
    for c in range(own):
        term = lax.dot_general(
            gathered[c], precond[c], (((1,), (1,)), ((), ())), precision=HIGHEST, preferred_element_type=F32
        )
        if sweep > 0:
            term = term - beta[...] * fresh[c]
        col_term[c] = term
        norm = norm + term * term
        whole = jnp.dot(term, precond[c], precision=HIGHEST, preferred_element_type=F32).astype(BF16)
        scaled[:, c] = jnp.broadcast_to(whole[None], (scaled.shape[0],) + whole.shape)
    packed = pack(jnp.sum(norm, axis=-1, keepdims=True), 0)
    scaled[:, own] = jnp.broadcast_to(packed[None], (scaled.shape[0],) + packed.shape)


def last_kernel(norms, row_term, before, alpha, beta_before, search, iterate, rhobar, phibar, precond, out, left):
    beta = jnp.sqrt(jnp.sum(norms[...], axis=0) + EPS)
    left[...] = row_term[...] * (1.0 / beta)[None]
    state = (before[...], search[...], iterate[...], rhobar[...], phibar[...])
    _, direction, solved, rho, phi = advance(state, alpha[...], beta_before[...])
    rotation = jnp.sqrt(rho * rho + beta * beta)
    solved = solved + ((rho / rotation) * phi / rotation) * direction
    for c in range(out.shape[0]):
        out[c] = jnp.dot(solved[c], precond[c], precision=HIGHEST, preferred_element_type=F32)


def call(kernel, out_shape, operands, scalars=0, scratch=(), name=None):
    return pl.pallas_call(
        kernel,
        out_shape=out_shape,
        in_specs=[SM] * scalars + [VM] * (len(operands) - scalars),
        out_specs=jax.tree.map(lambda _: VM, out_shape),
        scratch_shapes=list(scratch),
        compiler_params=params(),
        name=name,
    )(*operands)


def shards(blocks, block_row, block_col, right_sides, precond):
    rows, rhs, size = right_sides.shape
    own = precond.shape[0]
    devices = lax.axis_size("rows")
    chips = devices // 2
    half = chips * (own + 1)
    core = lax.rem(lax.axis_index("rows"), 2)
    here = core[None].astype(jnp.int32)
    owner = block_col // own
    spot = ((owner & 1) ^ core) * half + (owner >> 1) * (own + 1) + block_col % own
    same_core = [[2 * chip + c for chip in range(chips)] for c in range(2)]
    swap = [(d, d ^ 1) for d in range(devices)]

    def exchange(parts):
        return lax.all_to_all(parts, "rows", 0, 0, axis_index_groups=same_core, tiled=True)

    def core_swap(array):
        return lax.ppermute(array, "rows", swap)

    part = like((chips, own + 1, rhs, size), BF16)
    norm = like((rhs, size))
    field = like((own, rhs, size))
    row_field = like((rows, rhs, size))
    total = pltpu.VMEM((2 * half, rhs, size), F32)

    def scatter(kept, sent):
        arrived = core_swap(sent)
        return exchange((kept.astype(F32) + arrived.astype(F32)).astype(BF16))

    kept, sent = call(
        first_kernel, [part, part], (here, block_row, spot, right_sides, blocks), 3, [total], "first_backward"
    )
    row_term = right_sides
    col_term = alpha = beta = None
    state = []
    for sweep in range(ITERS + 1):
        chunks = scatter(kept, sent)
        carried = [] if sweep == 0 else [col_term, alpha, beta] + state
        if sweep == ITERS:
            finished = carried
        new = call(
            functools.partial(column_kernel, sweep),
            [field, norm, part] + ([] if sweep == 0 else [field, field, norm, norm]),
            (chunks, precond, *carried),
            name=f"columns_{sweep}",
        )
        col_term, beta, scaled = new[:3]
        state = list(new[3:])
        if sweep == ITERS:
            break
        mine = exchange(scaled)
        other = core_swap(mine)
        flat = (half, rhs, size)
        product = call(
            functools.partial(forward_kernel, own + 1),
            like((rows + 1, rhs, size), BF16),
            (block_row, spot, mine.reshape(flat), other.reshape(flat), blocks),
            2,
            [pltpu.VMEM((2 * half, rhs, size), F32), pltpu.VMEM((rows, rhs, size), F32)],
            f"forward_{sweep}",
        )
        crossed = lax.ppermute(product, "cols", [(0, 1), (1, 0)])
        if sweep < ITERS - 1:
            row_term, alpha, kept, sent = call(
                back_kernel,
                [row_field, norm, part, part],
                (here, block_row, spot, product, crossed, row_term, beta, blocks),
                3,
                [total],
                f"backward_{sweep}",
            )
        else:
            row_term, alpha, norms = call(
                finish_kernel,
                [row_field, norm, like((devices, rhs, size))],
                (product, crossed, row_term, beta),
                name="finish_rows",
            )
            kept, sent = call(
                first_kernel, [part, part], (here, block_row, spot, row_term, blocks), 3, [total], "last_backward"
            )
    norms = lax.all_to_all(norms, "rows", 0, 0, tiled=True)
    return call(last_kernel, [field, row_field], (norms, row_term, *finished, precond), name="last")


def solution(mesh):
    return jax.shard_map(
        shards,
        mesh=mesh,
        in_specs=(
            P(("rows", "cols"), None, None),
            P(("rows", "cols")),
            P(("rows", "cols")),
            P("rows", None, None),
            P(("cols", "rows"), None, None),
        ),
        out_specs=(P(("cols", "rows"), None, None), P("rows", None, None)),
        check_vma=False,
    )
```

```python
import functools

import jax
import jax.numpy as jnp
from jax import lax
from jax.experimental import pallas as pl
from jax.experimental.pallas import tpu as pltpu
from jax.sharding import PartitionSpec as P

ITERS = 3


EPS = 1e-06
F32 = jnp.float32
BF16 = jnp.bfloat16
VM = pl.BlockSpec(memory_space=pltpu.VMEM)
SM = pl.BlockSpec(memory_space=pltpu.SMEM)
LATE = 16


def params():
    return pltpu.CompilerParams(vmem_limit_bytes=16 << 20)


def like(shape, dtype=F32):
    return jax.ShapeDtypeStruct(shape, dtype)


def pack(total, first):
    half = total * 0.5
    top = half.astype(BF16).astype(F32)
    middle = (half - top).astype(BF16).astype(F32)
    low = half - top - middle
    lane = lax.broadcasted_iota(jnp.int32, (total.shape[0], 128), 1) - first
    terms = jnp.where(lane == 0, top, jnp.where(lane == 1, middle, jnp.where(lane == 2, low, 0.0)))
    return terms.astype(BF16)


def unpack(block):
    return jnp.sum(block, axis=-1, keepdims=True) * 2.0


def squares(field):
    return jnp.sum(jnp.sum(field * field, axis=0), axis=-1, keepdims=True)


def unroll_of(count):
    return next(u for u in (128, 64, 32, 16, 8, 4, 2) if count % u == 0)


def accumulate(products, source, target, table, blocks, total, arrive=None):
    count = blocks.shape[0]
    unroll = unroll_of(count)

    def add(base, pending):
        at, term = pending
        spot = target[base + at]
        total[spot] = total[spot] + term

    def step(i, carry):
        base = i * unroll
        if arrive is not None:
            arrive(i)
        pending = []
        for u in range(0, unroll, 2):
            pair = jnp.concatenate([table[source[base + u]], table[source[base + u + 1]]], axis=0)
            pending += list(zip((u, u + 1), products(pair, blocks[pl.ds(base + u, 2)])))
            while len(pending) > LATE:
                add(base, pending.pop(0))
        for item in pending:
            add(base, item)
        return carry

    lax.fori_loop(0, count // unroll, step, 0)


def forward_pair(pair, blocks):
    both = lax.dot_general(
        pair.astype(BF16),
        blocks.reshape(-1, blocks.shape[2]),
        (((1,), (1,)), ((), ())),
        preferred_element_type=F32,
    )
    size = blocks.shape[1]
    half = pair.shape[0] // 2
    return both[:half, :size], both[half:, size:]


def backward_pair(pair, blocks):
    half = pair.shape[0] // 2
    none = jnp.zeros((half, pair.shape[1]), F32)
    spread = jnp.concatenate(
        [jnp.concatenate([pair[:half], none], axis=1), jnp.concatenate([none, pair[half:]], axis=1)], axis=0
    )
    both = jnp.dot(spread.astype(BF16), blocks.reshape(-1, blocks.shape[2]), preferred_element_type=F32)
    return both[:half], both[half:]


def send_sums(here, row_term, row, spot, blocks, kept, sent, total, arrive=None):
    total[...] = jnp.zeros_like(total)
    accumulate(backward_pair, row, spot, row_term, blocks, total, arrive)
    half = kept.shape[0] * kept.shape[1]
    kept[...] = total[:half].astype(BF16).reshape(kept.shape)
    sent[...] = total[half:].astype(BF16).reshape(sent.shape)
    norm = pack(squares(row_term[...]), 3 * here[0])
    last = kept.shape[1] - 1
    for chip in range(kept.shape[0]):
        kept[chip, last] = norm
        sent[chip, last] = norm


def first_kernel(here, row, spot, right_sides, blocks, kept, sent, held, total, table, done):
    count = unroll_of(blocks.shape[0])
    parts = blocks.shape[0] // count

    def load(i):
        span = pl.ds(i * count, count)
        return pltpu.make_async_copy(blocks.at[span], held.at[span], done.at[i])

    right = pltpu.make_async_copy(right_sides, table, done.at[parts])
    right.start()
    for i in range(parts):
        load(i).start()
    right.wait()
    send_sums(here, table, row, spot, held, kept, sent, total, lambda i: load(i).wait())


def dead_kernel(here, row, spot, row_term, blocks, kept, sent, total):
    send_sums(here, row_term, row, spot, blocks, kept, sent, total)


def new_row_term(mine, other, before, beta, row_term, alpha):
    count = before.shape[0]
    norm = jnp.sqrt(unpack(mine[count].astype(F32)) + unpack(other[count].astype(F32)) + EPS)
    alpha[...] = jnp.broadcast_to(norm, alpha.shape)
    product = mine[:count].astype(F32) + other[:count].astype(F32)
    row_term[...] = product * (1.0 / alpha[...])[None] - before[...] * (alpha[...] / beta[...])[None]


def back_kernel(here, row, spot, mine, other, before, beta, blocks, row_term, alpha, kept, sent, total):
    new_row_term(mine, other, before, beta, row_term, alpha)
    send_sums(here, row_term, row, spot, blocks, kept, sent, total)


def diagonal(count):
    lanes = (count, 128)
    return lax.broadcasted_iota(jnp.int32, lanes, 0) == lax.broadcasted_iota(jnp.int32, lanes, 1)


def finish_kernel(mine, other, before, beta, row_term, alpha, norms):
    new_row_term(mine, other, before, beta, row_term, alpha)
    total = squares(row_term[...])
    flat = jnp.sum(jnp.where(diagonal(total.shape[0]), total, 0.0), axis=0, keepdims=True)
    norms[...] = jnp.broadcast_to(flat[None], norms.shape)


def forward_kernel(step, row, spot, mine, other, blocks, product, table, total):
    half = mine.shape[0]
    table[:half] = mine[...].astype(F32)
    table[half:] = other[...].astype(F32)
    total[...] = jnp.zeros_like(total)
    accumulate(forward_pair, spot, row, table, blocks, total)
    count = total.shape[0]
    product[:count] = total[...].astype(BF16)
    norm = jnp.zeros(total.shape[1:], F32)
    for last in range(step - 1, half, step):
        norm = norm + table[last] + table[half + last]
    product[count] = pack(unpack(norm), 0)


def advance(state, alpha, beta):
    col_term, search, iterate, rhobar, phibar = state
    fresh = col_term / alpha
    rotation = jnp.sqrt(rhobar * rhobar + beta * beta)
    cosine = rhobar / rotation
    sine = beta / rotation
    theta = sine * alpha
    phi = cosine * phibar
    iterate = iterate + (phi / rotation) * search
    search = fresh - (theta / rotation) * search
    return fresh, search, iterate, -cosine * alpha, sine * phibar


def times(field, high, low, side):
    top = field.astype(BF16)
    rest = (field - top.astype(F32)).astype(BF16)
    dims = (((1,), (side,)), ((), ()))
    both = lax.dot_general(jnp.concatenate([top, rest], axis=0), high, dims, preferred_element_type=F32)
    half = field.shape[0]
    return both[:half] + both[half:] + lax.dot_general(top, low, dims, preferred_element_type=F32)


def column_kernel(sweep, chunks, *refs):
    if sweep == 0:
        precond, col_term, beta, scaled, high, low = refs
        top = precond[...].astype(BF16)
        high[...] = top
        low[...] = (precond[...] - top.astype(F32)).astype(BF16)
    elif sweep == 1:
        high, low, before, alpha, beta_before, col_term, beta, scaled, search, iterate, rhobar, phibar = refs
        fresh = before[...] / alpha[...][None]
        search[...] = fresh
        iterate[...] = jnp.zeros_like(iterate)
        rhobar[...] = alpha[...]
        phibar[...] = beta_before[...]
    else:
        (high, low, before, alpha, beta_before, search_in, iterate_in, rhobar_in, phibar_in) = refs[:9]
        col_term, beta, scaled, search, iterate, rhobar, phibar = refs[9:]
        state = (before[...], search_in[...], iterate_in[...], rhobar_in[...], phibar_in[...])
        fresh, search[...], iterate[...], rhobar[...], phibar[...] = advance(state, alpha[...], beta_before[...])
    own = col_term.shape[0]
    gathered = jnp.sum(chunks[...].astype(F32), axis=0)
    beta[...] = jnp.broadcast_to(jnp.sqrt(unpack(gathered[own]) + EPS), beta.shape)
    gathered = gathered * (1.0 / beta[...])[None]
    terms = [times(gathered[c], high[c], low[c], 1) for c in range(own)]
    if sweep > 0:
        terms = [terms[c] - beta[...] * fresh[c] for c in range(own)]
    norm = sum(term * term for term in terms)
    wholes = [times(terms[c], high[c], low[c], 0).astype(BF16) for c in range(own)]
    for c in range(own):
        col_term[c] = terms[c]
        scaled[:, c] = jnp.broadcast_to(wholes[c][None], (scaled.shape[0],) + wholes[c].shape)
    packed = pack(jnp.sum(norm, axis=-1, keepdims=True), 0)
    scaled[:, own] = jnp.broadcast_to(packed[None], (scaled.shape[0],) + packed.shape)


def last_kernel(norms, row_term, high, low, before, alpha, beta_before, search, iterate, rhobar, phibar, out, left):
    flat = jnp.sum(norms[...], axis=0)
    total = jnp.sum(jnp.where(diagonal(alpha.shape[0]), flat, 0.0), axis=-1, keepdims=True)
    beta = jnp.broadcast_to(jnp.sqrt(total + EPS), alpha.shape)
    left[...] = row_term[...] * (1.0 / beta)[None]
    state = (before[...], search[...], iterate[...], rhobar[...], phibar[...])
    _, direction, solved, rho, phi = advance(state, alpha[...], beta_before[...])
    rotation = jnp.sqrt(rho * rho + beta * beta)
    solved = solved + ((rho / rotation) * phi / rotation) * direction
    for c in range(out.shape[0]):
        out[c] = times(solved[c], high[c], low[c], 0)


def call(kernel, out_shape, operands, scalars=0, scratch=(), name=None, space=pltpu.VMEM):
    return pl.pallas_call(
        kernel,
        out_shape=out_shape,
        in_specs=[SM] * scalars + [pl.BlockSpec(memory_space=space)] * (len(operands) - scalars),
        out_specs=jax.tree.map(lambda _: VM, out_shape),
        scratch_shapes=list(scratch),
        compiler_params=params(),
        name=name,
    )(*operands)


def shards(blocks, block_row, block_col, right_sides, precond):
    rows, rhs, size = right_sides.shape
    own = precond.shape[0]
    devices = lax.axis_size("rows")
    chips = devices // 2
    half = chips * (own + 1)
    core = lax.rem(lax.axis_index("rows"), 2)
    here = core[None].astype(jnp.int32)
    owner = block_col // own
    spot = ((owner & 1) ^ core) * half + (owner >> 1) * (own + 1) + block_col % own
    same_core = [[2 * chip + c for chip in range(chips)] for c in range(2)]
    swap = [(d, d ^ 1) for d in range(devices)]

    def exchange(parts):
        return lax.all_to_all(parts, "rows", 0, 0, axis_index_groups=same_core, tiled=True)

    def core_swap(array):
        return lax.ppermute(array, "rows", swap)

    part = like((chips, own + 1, rhs, size), BF16)
    norm = like((rhs, size))
    field = like((own, rhs, size))
    row_field = like((rows, rhs, size))
    total = pltpu.VMEM((2 * half, rhs, size), F32)

    def scatter(kept, sent):
        arrived = core_swap(sent)
        return exchange((kept.astype(F32) + arrived.astype(F32)).astype(BF16))

    kept, sent, held = call(
        first_kernel,
        [part, part, pltpu.VMEM(blocks.shape, BF16)],
        (here, block_row, spot, pltpu.with_memory_space_constraint(right_sides, pltpu.HBM), blocks),
        3,
        [
            total,
            pltpu.VMEM((rows, rhs, size), F32),
            pltpu.SemaphoreType.DMA((blocks.shape[0] // unroll_of(blocks.shape[0]) + 1,)),
        ],
        "first_backward",
        pl.ANY,
    )
    blocks = pltpu.with_memory_space_constraint(held, pltpu.VMEM)
    row_term = right_sides
    col_term = alpha = beta = None
    state = []
    for sweep in range(ITERS + 1):
        chunks = scatter(kept, sent)
        carried = [precond] if sweep == 0 else [high, low, col_term, alpha, beta] + state
        new = call(
            functools.partial(column_kernel, sweep),
            [field, norm, part] + ([like(precond.shape, BF16)] * 2 if sweep == 0 else [field, field, norm, norm]),
            (chunks, *carried),
            name=f"columns_{sweep}",
        )
        col_term, beta, scaled = new[:3]
        if sweep == ITERS:
            break
        if sweep == 0:
            high, low = new[3:]
        else:
            state = list(new[3:])
        mine = exchange(scaled)
        other = core_swap(mine)
        flat = (half, rhs, size)
        product = call(
            functools.partial(forward_kernel, own + 1),
            like((rows + 1, rhs, size), BF16),
            (block_row, spot, mine.reshape(flat), other.reshape(flat), blocks),
            2,
            [pltpu.VMEM((2 * half, rhs, size), F32), pltpu.VMEM((rows, rhs, size), F32)],
            f"forward_{sweep}",
        )
        crossed = lax.ppermute(product, "cols", [(0, 1), (1, 0)])
        if sweep < ITERS - 1:
            row_term, alpha, kept, sent = call(
                back_kernel,
                [row_field, norm, part, part],
                (here, block_row, spot, product, crossed, row_term, beta, blocks),
                3,
                [total],
                f"backward_{sweep}",
            )
        else:
            row_term, alpha, norms = call(
                finish_kernel,
                [row_field, norm, like((devices, 1, size))],
                (product, crossed, row_term, beta),
                name="finish_rows",
            )
            kept, sent = call(
                dead_kernel, [part, part], (here, block_row, spot, row_term, blocks), 3, [total], "last_backward"
            )
    norms = lax.all_to_all(norms, "rows", 0, 0, tiled=True)
    return call(last_kernel, [field, row_field], (norms, row_term, *carried), name="last")


def solution(mesh):
    return jax.shard_map(
        shards,
        mesh=mesh,
        in_specs=(
            P(("rows", "cols"), None, None),
            P(("rows", "cols")),
            P(("rows", "cols")),
            P("rows", None, None),
            P(("cols", "rows"), None, None),
        ),
        out_specs=(P(("cols", "rows"), None, None), P("rows", None, None)),
        check_vma=False,
    )
```

```python
import functools

import jax
import jax.numpy as jnp
from jax import lax
from jax.experimental import pallas as pl
from jax.experimental.pallas import tpu as pltpu
from jax.sharding import PartitionSpec as P

ITERS = 3


EPS = 1e-06
F32 = jnp.float32
BF16 = jnp.bfloat16
VM = pl.BlockSpec(memory_space=pltpu.VMEM)
SM = pl.BlockSpec(memory_space=pltpu.SMEM)
LATE = 16
AHEAD = 3
PLAIN = (1, 5)


def like(shape, dtype=F32):
    return jax.ShapeDtypeStruct(shape, dtype)


def pack(total, first):
    half = total * 0.5
    top = half.astype(BF16).astype(F32)
    middle = (half - top).astype(BF16).astype(F32)
    low = half - top - middle
    lane = lax.broadcasted_iota(jnp.int32, (total.shape[0], 128), 1) - first
    terms = jnp.where(lane == 0, top, jnp.where(lane == 1, middle, jnp.where(lane == 2, low, 0.0)))
    return terms.astype(BF16)


def unpack(block):
    return jnp.sum(block, axis=-1, keepdims=True) * 2.0


def squares(field):
    return jnp.sum(jnp.sum(field * field, axis=0), axis=-1, keepdims=True)


def part_of(whole, plain):
    return next(u for u in (64, 32, 16, 8, 4, 2) if whole % u == 0 and plain % u == 0)


def unroll_of(count, most):
    return next(u for u in (320, 160, 128, 64, 32, 16, 8, 4, 2) if u <= most and count % u == 0)


def accumulate(products, source, target, table, get, total, first, count, most=320, arrive=None, also=None):
    if count == 0:
        return
    unroll = unroll_of(count, most)

    def add(base, pending):
        at, term = pending
        spot = target(base + at)
        total[spot] = total[spot] + term

    def step(i, carry):
        base = first + i * unroll
        if arrive is not None:
            arrive(first // unroll + i)
        pending = []
        for u in range(0, unroll, 2):
            pair = jnp.concatenate([table[source(base + u)], table[source(base + u + 1)]], axis=0)
            if also is not None:
                also(base + u)
                also(base + u + 1)
            pending += list(zip((u, u + 1), products(pair, get(base + u))))
            while len(pending) > LATE:
                add(base, pending.pop(0))
        for item in pending:
            add(base, item)
        return carry

    lax.fori_loop(0, count // unroll, step, 0)


def turned_pair(pair, blocks):
    both = lax.dot_general(
        pair.astype(BF16),
        blocks.reshape(-1, blocks.shape[2]),
        (((1,), (1,)), ((), ())),
        preferred_element_type=F32,
    )
    size = blocks.shape[1]
    half = pair.shape[0] // 2
    return both[:half, :size], both[half:, size:]


def block_pair(pair, blocks):
    half = pair.shape[0] // 2
    none = jnp.zeros((half, pair.shape[1]), F32)
    spread = jnp.concatenate(
        [jnp.concatenate([pair[:half], none], axis=1), jnp.concatenate([none, pair[half:]], axis=1)], axis=0
    )
    both = jnp.dot(spread.astype(BF16), blocks.reshape(-1, blocks.shape[2]), preferred_element_type=F32)
    return both[:half], both[half:]


def finish_sums(here, row_term, kept, sent, total):
    half = kept.shape[0] * kept.shape[1]
    kept[...] = total[:half].astype(BF16).reshape(kept.shape)
    sent[...] = total[half:].astype(BF16).reshape(sent.shape)
    norm = pack(squares(row_term[...]), 3 * here[0])
    last = kept.shape[1] - 1
    for chip in range(kept.shape[0]):
        kept[chip, last] = norm
        sent[chip, last] = norm


def send_sums(here, row, spot, row_term, stored, kept, sent, total):
    count = row.shape[0]
    plain = stored.shape[0] - count
    total[...] = jnp.zeros_like(total)
    rows, spots = lambda n: row[n], lambda n: spot[n]
    accumulate(block_pair, rows, spots, row_term, lambda n: stored[pl.ds(count + n, 2)], total, 0, plain)
    accumulate(turned_pair, rows, spots, row_term, lambda n: stored[pl.ds(n, 2)], total, plain, count - plain)
    finish_sums(here, row_term, kept, sent, total)


def place(column, core, own, half):
    owner = column // own
    return ((owner & 1) ^ core) * half + (owner >> 1) * (own + 1) + column % own


def first_kernel(own, here, row_in, column_in, right_sides, blocks, kept, sent, stored, total, rest, table, row, column, done):
    whole = blocks.shape[0]
    plain = stored.shape[0] - whole
    count = part_of(whole, plain)
    half = kept.shape[0] * kept.shape[1]
    core = here[0]
    shift = own.bit_length() - 1

    def load(i, early):
        to = stored.at[pl.ds(whole + i * count, count)] if early else rest.at[pl.ds(i * count - plain, count)]
        return pltpu.make_async_copy(blocks.at[pl.ds(i * count, count)], to, done.at[i])

    def start(i):
        @pl.when(i < plain // count)
        def _():
            load(i, True).start()

        @pl.when((i >= plain // count) & (i < whole // count))
        def _():
            load(i, False).start()

    small = [
        pltpu.make_async_copy(a, b, done.at[whole // count + i])
        for i, (a, b) in enumerate(((row_in, row), (column_in, column), (right_sides, table)))
    ]
    for copy in small:
        copy.start()
    for i in range(AHEAD):
        start(i)

    def spot(n):
        if own != 1 << shift:
            return place(column[n], core, own, half)
        owner = lax.shift_right_logical(column[n], shift)
        chip = lax.shift_right_logical(owner, 1)
        return ((owner & 1) ^ core) * half + chip * (own + 1) + (column[n] & (own - 1))

    for copy in small:
        copy.wait()
    total[...] = jnp.zeros_like(total)
    for early, first, until in ((True, 0, plain), (False, plain, whole)):
        ref, shifted = (stored, whole) if early else (rest, -plain)

        def arrive(i, early=early):
            load(i, early).wait()
            start(i + AHEAD)

        def turn(n, ref=ref, shifted=shifted):
            stored[n] = ref[shifted + n].T

        def get(n, ref=ref, shifted=shifted):
            return ref[pl.ds(shifted + n, 2)]

        accumulate(
            block_pair, lambda n: row[n], spot, table, get, total, first, until - first, count, arrive, turn
        )
    finish_sums(here, table, kept, sent, total)


def place_kernel(own, half, here, column, spot):
    spot[...] = place(column[...], here[0], own, half)


def add_kernel(kept, arrived, both):
    both[...] = (kept[...].astype(F32) + arrived[...].astype(F32)).astype(BF16)


def dead_kernel(here, row, spot, row_term, stored, kept, sent, total):
    send_sums(here, row, spot, row_term, stored, kept, sent, total)


def new_row_term(mine, other, before, beta, row_term, alpha):
    count = before.shape[0]
    norm = jnp.sqrt(unpack(mine[count].astype(F32)) + unpack(other[count].astype(F32)) + EPS)
    alpha[...] = jnp.broadcast_to(norm, alpha.shape)
    product = mine[:count].astype(F32) + other[:count].astype(F32)
    row_term[...] = product * (1.0 / alpha[...])[None] - before[...] * (alpha[...] / beta[...])[None]


def back_kernel(here, row, spot, mine, other, before, beta, stored, row_term, alpha, kept, sent, total):
    new_row_term(mine, other, before, beta, row_term, alpha)
    send_sums(here, row, spot, row_term, stored, kept, sent, total)


def diagonal(count):
    lanes = (count, 128)
    return lax.broadcasted_iota(jnp.int32, lanes, 0) == lax.broadcasted_iota(jnp.int32, lanes, 1)


def finish_kernel(mine, other, before, beta, row_term, alpha, norms):
    new_row_term(mine, other, before, beta, row_term, alpha)
    total = squares(row_term[...])
    flat = jnp.sum(jnp.where(diagonal(total.shape[0]), total, 0.0), axis=0, keepdims=True)
    norms[...] = jnp.broadcast_to(flat[None], norms.shape)


def forward_kernel(step, row, spot, mine, other, stored, product, table, total):
    half = mine.shape[0]
    table[:half] = mine[...].astype(F32)
    table[half:] = other[...].astype(F32)
    total[...] = jnp.zeros_like(total)
    rows, spots = lambda n: row[n], lambda n: spot[n]
    accumulate(block_pair, spots, rows, table, lambda n: stored[pl.ds(n, 2)], total, 0, row.shape[0])
    count = total.shape[0]
    product[:count] = total[...].astype(BF16)
    norm = jnp.zeros(total.shape[1:], F32)
    for last in range(step - 1, half, step):
        norm = norm + table[last] + table[half + last]
    product[count] = pack(unpack(norm), 0)


def advance(state, alpha, beta):
    col_term, search, iterate, rhobar, phibar = state
    fresh = col_term / alpha
    rotation = jnp.sqrt(rhobar * rhobar + beta * beta)
    cosine = rhobar / rotation
    sine = beta / rotation
    theta = sine * alpha
    phi = cosine * phibar
    iterate = iterate + (phi / rotation) * search
    search = fresh - (theta / rotation) * search
    return fresh, search, iterate, -cosine * alpha, sine * phibar


def times(field, high, low, side):
    top = field.astype(BF16)
    rest = (field - top.astype(F32)).astype(BF16)
    dims = (((1,), (side,)), ((), ()))
    both = lax.dot_general(jnp.concatenate([top, rest], axis=0), high, dims, preferred_element_type=F32)
    half = field.shape[0]
    return both[:half] + both[half:] + lax.dot_general(top, low, dims, preferred_element_type=F32)


def column_kernel(sweep, chunks, *refs):
    if sweep == 0:
        precond, col_term, beta, scaled, high, low = refs
        top = precond[...].astype(BF16)
        high[...] = top
        low[...] = (precond[...] - top.astype(F32)).astype(BF16)
    elif sweep == 1:
        high, low, before, alpha, beta_before, col_term, beta, scaled, search, iterate, rhobar, phibar = refs
        fresh = before[...] / alpha[...][None]
        search[...] = fresh
        iterate[...] = jnp.zeros_like(iterate)
        rhobar[...] = alpha[...]
        phibar[...] = beta_before[...]
    else:
        (high, low, before, alpha, beta_before, search_in, iterate_in, rhobar_in, phibar_in) = refs[:9]
        col_term, beta, scaled, search, iterate, rhobar, phibar = refs[9:]
        state = (before[...], search_in[...], iterate_in[...], rhobar_in[...], phibar_in[...])
        fresh, search[...], iterate[...], rhobar[...], phibar[...] = advance(state, alpha[...], beta_before[...])
    own = col_term.shape[0]
    gathered = jnp.sum(chunks[...].astype(F32), axis=0)
    beta[...] = jnp.broadcast_to(jnp.sqrt(unpack(gathered[own]) + EPS), beta.shape)
    gathered = gathered * (1.0 / beta[...])[None]
    terms = [times(gathered[c], high[c], low[c], 1) for c in range(own)]
    if sweep > 0:
        terms = [terms[c] - beta[...] * fresh[c] for c in range(own)]
    norm = sum(term * term for term in terms)
    wholes = [times(terms[c], high[c], low[c], 0).astype(BF16) for c in range(own)]
    for c in range(own):
        col_term[c] = terms[c]
        scaled[:, c] = jnp.broadcast_to(wholes[c][None], (scaled.shape[0],) + wholes[c].shape)
    packed = pack(jnp.sum(norm, axis=-1, keepdims=True), 0)
    scaled[:, own] = jnp.broadcast_to(packed[None], (scaled.shape[0],) + packed.shape)


def last_kernel(norms, row_term, high, low, before, alpha, beta_before, search, iterate, rhobar, phibar, out, left):
    flat = jnp.sum(norms[...], axis=0)
    total = jnp.sum(jnp.where(diagonal(alpha.shape[0]), flat, 0.0), axis=-1, keepdims=True)
    beta = jnp.broadcast_to(jnp.sqrt(total + EPS), alpha.shape)
    left[...] = row_term[...] * (1.0 / beta)[None]
    state = (before[...], search[...], iterate[...], rhobar[...], phibar[...])
    _, direction, solved, rho, phi = advance(state, alpha[...], beta_before[...])
    rotation = jnp.sqrt(rho * rho + beta * beta)
    solved = solved + ((rho / rotation) * phi / rotation) * direction
    for c in range(out.shape[0]):
        out[c] = times(solved[c], high[c], low[c], 0)


def call(kernel, out_shape, operands, scalars=0, scratch=(), name=None, space=pltpu.VMEM, room=8):
    return pl.pallas_call(
        kernel,
        out_shape=out_shape,
        in_specs=[SM] * scalars + [pl.BlockSpec(memory_space=space)] * (len(operands) - scalars),
        out_specs=jax.tree.map(lambda _: VM, out_shape),
        scratch_shapes=list(scratch),
        compiler_params=pltpu.CompilerParams(vmem_limit_bytes=room << 20),
        name=name,
    )(*operands)


def shards(blocks, block_row, block_col, right_sides, precond):
    rows, rhs, size = right_sides.shape
    own = precond.shape[0]
    devices = lax.axis_size("rows")
    chips = devices // 2
    half = chips * (own + 1)
    core = lax.rem(lax.axis_index("rows"), 2)
    here = core[None].astype(jnp.int32)
    spot = call(
        functools.partial(place_kernel, own, half), like(block_col.shape, jnp.int32), (here, block_col), 1, name="place"
    )
    same_core = [[2 * chip + c for chip in range(chips)] for c in range(2)]
    swap = [(d, d ^ 1) for d in range(devices)]

    def exchange(parts):
        return lax.all_to_all(parts, "rows", 0, 0, axis_index_groups=same_core, tiled=True)

    def core_swap(array):
        return lax.ppermute(array, "rows", swap)

    part = like((chips, own + 1, rhs, size), BF16)
    norm = like((rhs, size))
    field = like((own, rhs, size))
    row_field = like((rows, rhs, size))
    total = pltpu.VMEM((2 * half, rhs, size), F32)

    def scatter(kept, sent):
        return exchange(call(add_kernel, part, (kept, core_swap(sent)), name="add_cores"))

    in_hbm = [pltpu.with_memory_space_constraint(a, pltpu.HBM) for a in (block_row, block_col, right_sides, blocks)]
    count = blocks.shape[0]
    plain = count * PLAIN[0] // PLAIN[1] // 2 * 2
    kept, sent, stored = call(
        functools.partial(first_kernel, own),
        [part, part, pltpu.VMEM((count + plain,) + blocks.shape[1:], BF16)],
        (here, *in_hbm),
        1,
        [
            total,
            pltpu.VMEM((count - plain,) + blocks.shape[1:], BF16),
            pltpu.VMEM((rows, rhs, size), F32),
            pltpu.SMEM(block_row.shape, jnp.int32),
            pltpu.SMEM(block_col.shape, jnp.int32),
            pltpu.SemaphoreType.DMA((count // part_of(count, plain) + 3,)),
        ],
        "first_backward",
        pl.ANY,
        7 + (2 * (count - plain) * size * size >> 20),
    )
    stored = pltpu.with_memory_space_constraint(stored, pltpu.VMEM)
    row_term = right_sides
    col_term = alpha = beta = None
    state = []
    for sweep in range(ITERS + 1):
        chunks = scatter(kept, sent)
        carried = [precond] if sweep == 0 else [high, low, col_term, alpha, beta] + state
        new = call(
            functools.partial(column_kernel, sweep),
            [field, norm, part] + ([like(precond.shape, BF16)] * 2 if sweep == 0 else [field, field, norm, norm]),
            (chunks, *carried),
            name=f"columns_{sweep}",
        )
        col_term, beta, scaled = new[:3]
        if sweep == ITERS:
            break
        if sweep == 0:
            high, low = new[3:]
        else:
            state = list(new[3:])
        mine = exchange(scaled)
        other = core_swap(mine)
        flat = (half, rhs, size)
        product = call(
            functools.partial(forward_kernel, own + 1),
            like((rows + 1, rhs, size), BF16),
            (block_row, spot, mine.reshape(flat), other.reshape(flat), stored),
            2,
            [pltpu.VMEM((2 * half, rhs, size), F32), pltpu.VMEM((rows, rhs, size), F32)],
            f"forward_{sweep}",
        )
        crossed = lax.ppermute(product, "cols", [(0, 1), (1, 0)])
        if sweep < ITERS - 1:
            row_term, alpha, kept, sent = call(
                back_kernel,
                [row_field, norm, part, part],
                (here, block_row, spot, product, crossed, row_term, beta, stored),
                3,
                [total],
                f"backward_{sweep}",
            )
        else:
            row_term, alpha, norms = call(
                finish_kernel,
                [row_field, norm, like((devices, 1, size))],
                (product, crossed, row_term, beta),
                name="finish_rows",
            )
            kept, sent = call(
                dead_kernel, [part, part], (here, block_row, spot, row_term, stored), 3, [total], "last_backward"
            )
    norms = lax.all_to_all(norms, "rows", 0, 0, tiled=True)
    return call(last_kernel, [field, row_field], (norms, row_term, *carried), name="last")


def solution(mesh):
    return jax.shard_map(
        shards,
        mesh=mesh,
        in_specs=(
            P(("rows", "cols"), None, None),
            P(("rows", "cols")),
            P(("rows", "cols")),
            P("rows", None, None),
            P(("cols", "rows"), None, None),
        ),
        out_specs=(P(("cols", "rows"), None, None), P("rows", None, None)),
        check_vma=False,
    )
```

```python
import functools

import jax
import jax.numpy as jnp
from jax import lax
from jax.experimental import pallas as pl
from jax.experimental.pallas import tpu as pltpu
from jax.sharding import PartitionSpec as P

ITERS = 3


EPS = 1e-06
F32 = jnp.float32
BF16 = jnp.bfloat16
VM = pl.BlockSpec(memory_space=pltpu.VMEM)
SM = pl.BlockSpec(memory_space=pltpu.SMEM)
LATE = 16
AHEAD = 3
PLAIN = (0, 1)


def like(shape, dtype=F32):
    return jax.ShapeDtypeStruct(shape, dtype)


def pack(total, first):
    half = total * 0.5
    top = half.astype(BF16).astype(F32)
    middle = (half - top).astype(BF16).astype(F32)
    low = half - top - middle
    lane = lax.broadcasted_iota(jnp.int32, (total.shape[0], 128), 1) - first
    terms = jnp.where(lane == 0, top, jnp.where(lane == 1, middle, jnp.where(lane == 2, low, 0.0)))
    return terms.astype(BF16)


def unpack(block):
    return jnp.sum(block, axis=-1, keepdims=True) * 2.0


def squares(field):
    return jnp.sum(jnp.sum(field * field, axis=0), axis=-1, keepdims=True)


def part_of(whole, plain):
    return next(u for u in (64, 32, 16, 8, 4, 2) if whole % u == 0 and plain % u == 0)


def unroll_of(count, most):
    return next(u for u in (640, 320, 160, 128, 64, 32, 16, 8, 4, 2) if u <= most and count % u == 0)


def accumulate(products, source, target, table, get, total, first, count, most=640, arrive=None, also=None):
    if count == 0:
        return
    unroll = unroll_of(count, most)

    def add(base, pending):
        at, term = pending
        spot = target(base + at)
        total[spot] = total[spot] + term

    def step(i, carry):
        base = first + i * unroll
        if arrive is not None:
            arrive(first // unroll + i)
        pending = []
        for u in range(0, unroll, 2):
            pair = jnp.concatenate([table[source(base + u)], table[source(base + u + 1)]], axis=0)
            if also is not None:
                also(base + u)
                also(base + u + 1)
            pending += list(zip((u, u + 1), products(pair, get(base + u))))
            while len(pending) > LATE:
                add(base, pending.pop(0))
        for item in pending:
            add(base, item)
        return carry

    lax.fori_loop(0, count // unroll, step, 0)


def block_pair(pair, blocks):
    half = pair.shape[0] // 2
    none = jnp.zeros((half, pair.shape[1]), F32)
    spread = jnp.concatenate(
        [jnp.concatenate([pair[:half], none], axis=1), jnp.concatenate([none, pair[half:]], axis=1)], axis=0
    )
    both = jnp.dot(spread.astype(BF16), blocks.reshape(-1, blocks.shape[2]), preferred_element_type=F32)
    return both[:half], both[half:]


def finish_sums(here, row_term, kept, sent, total):
    half = kept.shape[0] * kept.shape[1]
    kept[...] = total[:half].astype(BF16).reshape(kept.shape)
    sent[...] = total[half:].astype(BF16).reshape(sent.shape)
    norm = pack(squares(row_term[...]), 3 * here[0])
    last = kept.shape[1] - 1
    for chip in range(kept.shape[0]):
        kept[chip, last] = norm
        sent[chip, last] = norm


def send_sums(here, row, spot, row_term, blocks, kept, sent, total):
    total[...] = jnp.zeros_like(total)
    get = lambda n: blocks[pl.ds(n, 2)]
    accumulate(block_pair, lambda n: row[n], lambda n: spot[n], row_term, get, total, 0, row.shape[0])
    finish_sums(here, row_term, kept, sent, total)


def load_kernel(blocks, after, loaded, done):
    parts = done.shape[0]
    count = blocks.shape[0] // parts
    copies = [
        pltpu.make_async_copy(blocks.at[pl.ds(i * count, count)], loaded.at[pl.ds(i * count, count)], done.at[i])
        for i in range(parts)
    ]
    for copy in copies:
        copy.start()
    for copy in copies:
        copy.wait()


def place(column, core, own, half):
    owner = column // own
    return ((owner & 1) ^ core) * half + (owner >> 1) * (own + 1) + column % own


def first_kernel(own, here, row_in, column_in, right_sides, blocks, kept, sent, stored, total, rest, table, row, column, done):
    whole = blocks.shape[0]
    plain = stored.shape[0] - whole
    count = part_of(whole, plain)
    half = kept.shape[0] * kept.shape[1]
    core = here[0]
    shift = own.bit_length() - 1

    def load(i, early):
        to = stored.at[pl.ds(whole + i * count, count)] if early else rest.at[pl.ds(i * count - plain, count)]
        return pltpu.make_async_copy(blocks.at[pl.ds(i * count, count)], to, done.at[i])

    def start(i):
        @pl.when(i < plain // count)
        def _():
            load(i, True).start()

        @pl.when((i >= plain // count) & (i < whole // count))
        def _():
            load(i, False).start()

    small = [
        pltpu.make_async_copy(a, b, done.at[whole // count + i])
        for i, (a, b) in enumerate(((row_in, row), (column_in, column), (right_sides, table)))
    ]
    for copy in small:
        copy.start()
    for i in range(AHEAD):
        start(i)

    def spot(n):
        if own != 1 << shift:
            return place(column[n], core, own, half)
        owner = lax.shift_right_logical(column[n], shift)
        chip = lax.shift_right_logical(owner, 1)
        return ((owner & 1) ^ core) * half + chip * (own + 1) + (column[n] & (own - 1))

    for copy in small:
        copy.wait()
    total[...] = jnp.zeros_like(total)
    for early, first, until in ((True, 0, plain), (False, plain, whole)):
        ref, shifted = (stored, whole) if early else (rest, -plain)

        def arrive(i, early=early):
            load(i, early).wait()
            start(i + AHEAD)

        def turn(n, ref=ref, shifted=shifted):
            stored[n] = ref[shifted + n].T

        def get(n, ref=ref, shifted=shifted):
            return ref[pl.ds(shifted + n, 2)]

        accumulate(
            block_pair, lambda n: row[n], spot, table, get, total, first, until - first, count, arrive, turn
        )
    finish_sums(here, table, kept, sent, total)


def place_kernel(own, half, here, column, spot):
    spot[...] = place(column[...], here[0], own, half)


def add_kernel(kept, arrived, both):
    both[...] = (kept[...].astype(F32) + arrived[...].astype(F32)).astype(BF16)


def dead_kernel(here, row, spot, row_term, blocks, kept, sent, total):
    send_sums(here, row, spot, row_term, blocks, kept, sent, total)


def new_row_term(mine, other, before, beta, row_term, alpha):
    count = before.shape[0]
    norm = jnp.sqrt(unpack(mine[count].astype(F32)) + unpack(other[count].astype(F32)) + EPS)
    alpha[...] = jnp.broadcast_to(norm, alpha.shape)
    product = mine[:count].astype(F32) + other[:count].astype(F32)
    row_term[...] = product * (1.0 / alpha[...])[None] - before[...] * (alpha[...] / beta[...])[None]


def back_kernel(here, row, spot, mine, other, before, beta, blocks, row_term, alpha, kept, sent, total):
    new_row_term(mine, other, before, beta, row_term, alpha)
    send_sums(here, row, spot, row_term, blocks, kept, sent, total)


def diagonal(count):
    lanes = (count, 128)
    return lax.broadcasted_iota(jnp.int32, lanes, 0) == lax.broadcasted_iota(jnp.int32, lanes, 1)


def finish_kernel(mine, other, before, beta, after, row_term, alpha, norms):
    new_row_term(mine, other, before, beta, row_term, alpha)
    total = squares(row_term[...])
    flat = jnp.sum(jnp.where(diagonal(total.shape[0]), total, 0.0), axis=0, keepdims=True)
    norms[...] = jnp.broadcast_to(flat[None], norms.shape)


def forward_kernel(step, row, spot, mine, other, stored, product, table, total):
    half = mine.shape[0]
    table[:half] = mine[...].astype(F32)
    table[half:] = other[...].astype(F32)
    total[...] = jnp.zeros_like(total)
    rows, spots = lambda n: row[n], lambda n: spot[n]
    accumulate(block_pair, spots, rows, table, lambda n: stored[pl.ds(n, 2)], total, 0, row.shape[0])
    count = total.shape[0]
    product[:count] = total[...].astype(BF16)
    norm = jnp.zeros(total.shape[1:], F32)
    for last in range(step - 1, half, step):
        norm = norm + table[last] + table[half + last]
    product[count] = pack(unpack(norm), 0)


def advance(state, alpha, beta):
    col_term, search, iterate, rhobar, phibar = state
    fresh = col_term / alpha
    rotation = jnp.sqrt(rhobar * rhobar + beta * beta)
    cosine = rhobar / rotation
    sine = beta / rotation
    theta = sine * alpha
    phi = cosine * phibar
    iterate = iterate + (phi / rotation) * search
    search = fresh - (theta / rotation) * search
    return fresh, search, iterate, -cosine * alpha, sine * phibar


def times(field, high, low, side):
    top = field.astype(BF16)
    rest = (field - top.astype(F32)).astype(BF16)
    dims = (((1,), (side,)), ((), ()))
    both = lax.dot_general(jnp.concatenate([top, rest], axis=0), high, dims, preferred_element_type=F32)
    half = field.shape[0]
    return both[:half] + both[half:] + lax.dot_general(top, low, dims, preferred_element_type=F32)


def column_kernel(sweep, chunks, *refs):
    if sweep == 0:
        precond, col_term, beta, scaled, high, low = refs
        top = precond[...].astype(BF16)
        high[...] = top
        low[...] = (precond[...] - top.astype(F32)).astype(BF16)
    elif sweep == 1:
        high, low, before, alpha, beta_before, col_term, beta, scaled, search, iterate, rhobar, phibar = refs
        fresh = before[...] / alpha[...][None]
        search[...] = fresh
        iterate[...] = jnp.zeros_like(iterate)
        rhobar[...] = alpha[...]
        phibar[...] = beta_before[...]
    else:
        (high, low, before, alpha, beta_before, search_in, iterate_in, rhobar_in, phibar_in) = refs[:9]
        col_term, beta, scaled, search, iterate, rhobar, phibar = refs[9:]
        state = (before[...], search_in[...], iterate_in[...], rhobar_in[...], phibar_in[...])
        fresh, search[...], iterate[...], rhobar[...], phibar[...] = advance(state, alpha[...], beta_before[...])
    own = col_term.shape[0]
    gathered = jnp.sum(chunks[...].astype(F32), axis=0)
    beta[...] = jnp.broadcast_to(jnp.sqrt(unpack(gathered[own]) + EPS), beta.shape)
    gathered = gathered * (1.0 / beta[...])[None]
    terms = [times(gathered[c], high[c], low[c], 1) for c in range(own)]
    if sweep > 0:
        terms = [terms[c] - beta[...] * fresh[c] for c in range(own)]
    norm = sum(term * term for term in terms)
    wholes = [times(terms[c], high[c], low[c], 0).astype(BF16) for c in range(own)]
    for c in range(own):
        col_term[c] = terms[c]
        scaled[:, c] = jnp.broadcast_to(wholes[c][None], (scaled.shape[0],) + wholes[c].shape)
    packed = pack(jnp.sum(norm, axis=-1, keepdims=True), 0)
    scaled[:, own] = jnp.broadcast_to(packed[None], (scaled.shape[0],) + packed.shape)


def prepare_kernel(after, high, low, *refs):
    half = len(refs) // 2
    for field, out in zip(refs[:half], refs[half:]):
        for c in range(field.shape[0]):
            out[c] = times(field[c], high[c], low[c], 0)


def last_kernel(norms, row_term, before, search, iterate, alpha, beta_before, rhobar, phibar, out, left):
    flat = jnp.sum(norms[...], axis=0)
    total = jnp.sum(jnp.where(diagonal(alpha.shape[0]), flat, 0.0), axis=-1, keepdims=True)
    beta = jnp.broadcast_to(jnp.sqrt(total + EPS), alpha.shape)
    left[...] = row_term[...] * (1.0 / beta)[None]
    state = (before[...], search[...], iterate[...], rhobar[...], phibar[...])
    _, direction, solved, rho, phi = advance(state, alpha[...], beta_before[...])
    rotation = jnp.sqrt(rho * rho + beta * beta)
    out[...] = solved + ((rho / rotation) * phi / rotation) * direction


def call(kernel, out_shape, operands, scalars=0, scratch=(), name=None, space=pltpu.VMEM, room=8, cost=None):
    return pl.pallas_call(
        kernel,
        out_shape=out_shape,
        in_specs=[SM] * scalars + [pl.BlockSpec(memory_space=space)] * (len(operands) - scalars),
        out_specs=jax.tree.map(lambda _: VM, out_shape),
        scratch_shapes=list(scratch),
        compiler_params=pltpu.CompilerParams(vmem_limit_bytes=room << 20),
        cost_estimate=cost,
        name=name,
    )(*operands)


def shards(blocks, block_row, block_col, right_sides, precond):
    rows, rhs, size = right_sides.shape
    own = precond.shape[0]
    devices = lax.axis_size("rows")
    chips = devices // 2
    half = chips * (own + 1)
    core = lax.rem(lax.axis_index("rows"), 2)
    here = core[None].astype(jnp.int32)
    spot = call(
        functools.partial(place_kernel, own, half), like(block_col.shape, jnp.int32), (here, block_col), 1, name="place"
    )
    same_core = [[2 * chip + c for chip in range(chips)] for c in range(2)]
    swap = [(d, d ^ 1) for d in range(devices)]

    def exchange(parts):
        return lax.all_to_all(parts, "rows", 0, 0, axis_index_groups=same_core, tiled=True)

    def core_swap(array):
        return lax.ppermute(array, "rows", swap)

    part = like((chips, own + 1, rhs, size), BF16)
    norm = like((rhs, size))
    field = like((own, rhs, size))
    row_field = like((rows, rhs, size))
    total = pltpu.VMEM((2 * half, rhs, size), F32)

    def scatter(kept, sent):
        return exchange(call(add_kernel, part, (kept, core_swap(sent)), name="add_cores"))

    in_hbm = [pltpu.with_memory_space_constraint(a, pltpu.HBM) for a in (block_row, block_col, right_sides, blocks)]
    count = blocks.shape[0]
    plain = count * PLAIN[0] // PLAIN[1] // 2 * 2
    kept, sent, stored = call(
        functools.partial(first_kernel, own),
        [part, part, pltpu.VMEM((count + plain,) + blocks.shape[1:], BF16)],
        (here, *in_hbm),
        1,
        [
            total,
            pltpu.VMEM((count - plain,) + blocks.shape[1:], BF16),
            pltpu.VMEM((rows, rhs, size), F32),
            pltpu.SMEM(block_row.shape, jnp.int32),
            pltpu.SMEM(block_col.shape, jnp.int32),
            pltpu.SemaphoreType.DMA((count // part_of(count, plain) + 3,)),
        ],
        "first_backward",
        pl.ANY,
        7 + (2 * (count - plain) * size * size >> 20),
    )
    stored = pltpu.with_memory_space_constraint(stored, pltpu.VMEM)
    row_term = right_sides
    col_term = alpha = beta = None
    state = []
    for sweep in range(ITERS + 1):
        chunks = scatter(kept, sent)
        carried = [precond] if sweep == 0 else [high, low, col_term, alpha, beta] + state
        new = call(
            functools.partial(column_kernel, sweep),
            [field, norm, part] + ([like(precond.shape, BF16)] * 2 if sweep == 0 else [field, field, norm, norm]),
            (chunks, *carried),
            name=f"columns_{sweep}",
        )
        col_term, beta, scaled = new[:3]
        if sweep == ITERS:
            break
        if sweep == 0:
            high, low = new[3:]
        else:
            state = list(new[3:])
        mine = exchange(scaled)
        other = core_swap(mine)
        flat = (half, rhs, size)
        product = call(
            functools.partial(forward_kernel, own + 1),
            like((rows + 1, rhs, size), BF16),
            (block_row, spot, mine.reshape(flat), other.reshape(flat), stored),
            2,
            [pltpu.VMEM((2 * half, rhs, size), F32), pltpu.VMEM((rows, rhs, size), F32)],
            f"forward_{sweep}",
        )
        crossed = lax.ppermute(product, "cols", [(0, 1), (1, 0)])
        loaded = call(
            load_kernel,
            pltpu.VMEM(blocks.shape, BF16),
            (in_hbm[3], product),
            0,
            [pltpu.SemaphoreType.DMA((unroll_of(count, 8),))],
            f"load_{sweep}",
            pl.ANY,
            1,
            pl.CostEstimate(flops=0, bytes_accessed=4 * count * size * size, transcendentals=0),
        )
        loaded = pltpu.with_memory_space_constraint(loaded, pltpu.VMEM)
        if sweep < ITERS - 1:
            row_term, alpha, kept, sent = call(
                back_kernel,
                [row_field, norm, part, part],
                (here, block_row, spot, product, crossed, row_term, beta, loaded),
                3,
                [total],
                f"backward_{sweep}",
            )
        else:
            search, iterate, rhobar, phibar = state
            fields = (col_term, search, iterate)
            ready = call(prepare_kernel, [field] * 3, (product, high, low, *fields), name="prepare")
            row_term, alpha, norms = call(
                finish_kernel,
                [row_field, norm, like((devices, 1, size))],
                (product, crossed, row_term, beta, ready[0]),
                name="finish_rows",
            )
            factors = (alpha, beta, rhobar, phibar)
            kept, sent = call(
                dead_kernel, [part, part], (here, block_row, spot, row_term, loaded), 3, [total], "last_backward"
            )
    norms = lax.all_to_all(norms, "rows", 0, 0, tiled=True)
    return call(last_kernel, [field, row_field], (norms, row_term, *ready, *factors), name="last")


def solution(mesh):
    return jax.shard_map(
        shards,
        mesh=mesh,
        in_specs=(
            P(("rows", "cols"), None, None),
            P(("rows", "cols")),
            P(("rows", "cols")),
            P("rows", None, None),
            P(("cols", "rows"), None, None),
        ),
        out_specs=(P(("cols", "rows"), None, None), P("rows", None, None)),
        check_vma=False,
    )
```

```python
import functools

import jax
import jax.numpy as jnp
from jax import lax
from jax.experimental import pallas as pl
from jax.experimental.pallas import tpu as pltpu
from jax.sharding import PartitionSpec as P

ITERS = 3


EPS = 1e-06
F32 = jnp.float32
BF16 = jnp.bfloat16
VM = pl.BlockSpec(memory_space=pltpu.VMEM)
SM = pl.BlockSpec(memory_space=pltpu.SMEM)
LATE = 16
AHEAD = 3
PLAIN = (0, 1)


def like(shape, dtype=F32):
    return jax.ShapeDtypeStruct(shape, dtype)


def pack(total, first):
    half = total * 0.5
    top = half.astype(BF16).astype(F32)
    middle = (half - top).astype(BF16).astype(F32)
    low = half - top - middle
    lane = lax.broadcasted_iota(jnp.int32, (total.shape[0], 128), 1) - first
    terms = jnp.where(lane == 0, top, jnp.where(lane == 1, middle, jnp.where(lane == 2, low, 0.0)))
    return terms.astype(BF16)


def unpack(block):
    return jnp.sum(block, axis=-1, keepdims=True) * 2.0


def squares(field):
    return jnp.sum(jnp.sum(field * field, axis=0), axis=-1, keepdims=True)


def part_of(whole, plain):
    return next(u for u in (64, 32, 16, 8, 4, 2) if whole % u == 0 and plain % u == 0)


def unroll_of(count, most):
    return next(u for u in (640, 320, 160, 128, 64, 32, 16, 8, 4, 2) if u <= most and count % u == 0)


def accumulate(products, pick, target, get, total, first, count, most=640, arrive=None, also=None):
    if count == 0:
        return
    unroll = unroll_of(count, most)

    def add(base, pending):
        at, term = pending
        spot = target(base + at)
        total[spot] = total[spot] + term

    def step(i, carry):
        base = first + i * unroll
        if arrive is not None:
            arrive(first // unroll + i)
        pending = []
        for u in range(0, unroll, 2):
            pair = jnp.concatenate([pick(base + u), pick(base + u + 1)], axis=0)
            if also is not None:
                also(base + u)
                also(base + u + 1)
            pending += list(zip((u, u + 1), products(pair, get(base + u))))
            while len(pending) > LATE:
                add(base, pending.pop(0))
        for item in pending:
            add(base, item)
        return carry

    lax.fori_loop(0, count // unroll, step, 0)


def block_pair(pair, blocks):
    half = pair.shape[0] // 2
    none = jnp.zeros((half, pair.shape[1]), F32)
    spread = jnp.concatenate(
        [jnp.concatenate([pair[:half], none], axis=1), jnp.concatenate([none, pair[half:]], axis=1)], axis=0
    )
    both = jnp.dot(spread.astype(BF16), blocks.reshape(-1, blocks.shape[2]), preferred_element_type=F32)
    return both[:half], both[half:]


def finish_sums(here, row_term, sent, total):
    half = sent.shape[0] * sent.shape[1]
    sent[...] = total[half:].astype(BF16).reshape(sent.shape)
    norm = pack(squares(row_term[...]), 3 * here[0])
    step = sent.shape[1]
    for chip in range(sent.shape[0]):
        total[chip * step + step - 1] = norm.astype(F32)
        sent[chip, step - 1] = norm


def send_sums(here, row, spot, row_term, blocks, total, sent):
    total[...] = jnp.zeros_like(total)
    get = lambda n: blocks[pl.ds(n, 2)]
    accumulate(block_pair, lambda n: row_term[row[n]], lambda n: spot[n], get, total, 0, row.shape[0])
    finish_sums(here, row_term, sent, total)


def load_kernel(blocks, after, loaded, done):
    parts = done.shape[0]
    count = blocks.shape[0] // parts
    copies = [
        pltpu.make_async_copy(blocks.at[pl.ds(i * count, count)], loaded.at[pl.ds(i * count, count)], done.at[i])
        for i in range(parts)
    ]
    for copy in copies:
        copy.start()
    for copy in copies:
        copy.wait()


def place(column, core, own, half):
    owner = column // own
    return ((owner & 1) ^ core) * half + (owner >> 1) * (own + 1) + column % own


def first_kernel(own, here, row_in, column_in, right_sides, blocks, total, sent, stored, rest, table, row, column, done):
    whole = blocks.shape[0]
    plain = stored.shape[0] - whole
    count = part_of(whole, plain)
    half = sent.shape[0] * sent.shape[1]
    core = here[0]
    shift = own.bit_length() - 1

    def load(i, early):
        to = stored.at[pl.ds(whole + i * count, count)] if early else rest.at[pl.ds(i * count - plain, count)]
        return pltpu.make_async_copy(blocks.at[pl.ds(i * count, count)], to, done.at[i])

    def start(i):
        @pl.when(i < plain // count)
        def _():
            load(i, True).start()

        @pl.when((i >= plain // count) & (i < whole // count))
        def _():
            load(i, False).start()

    small = [
        pltpu.make_async_copy(a, b, done.at[whole // count + i])
        for i, (a, b) in enumerate(((row_in, row), (column_in, column), (right_sides, table)))
    ]
    for copy in small:
        copy.start()
    for i in range(AHEAD):
        start(i)

    def spot(n):
        if own != 1 << shift:
            return place(column[n], core, own, half)
        owner = lax.shift_right_logical(column[n], shift)
        chip = lax.shift_right_logical(owner, 1)
        return ((owner & 1) ^ core) * half + chip * (own + 1) + (column[n] & (own - 1))

    for copy in small:
        copy.wait()
    total[...] = jnp.zeros_like(total)
    for early, first, until in ((True, 0, plain), (False, plain, whole)):
        ref, shifted = (stored, whole) if early else (rest, -plain)

        def arrive(i, early=early):
            load(i, early).wait()
            start(i + AHEAD)

        def turn(n, ref=ref, shifted=shifted):
            stored[n] = ref[shifted + n].T

        def get(n, ref=ref, shifted=shifted):
            return ref[pl.ds(shifted + n, 2)]

        accumulate(
            block_pair, lambda n: table[row[n]], spot, get, total, first, until - first, count, arrive, turn
        )
    finish_sums(here, table, sent, total)


def place_kernel(own, half, here, column, spot):
    spot[...] = place(column[...], here[0], own, half)


def add_kernel(total, arrived, both):
    half = both.shape[0] * both.shape[1]
    both[...] = (total[:half].reshape(both.shape) + arrived[...].astype(F32)).astype(BF16)


def dead_kernel(here, row, spot, row_term, blocks, total, sent):
    send_sums(here, row, spot, row_term, blocks, total, sent)


def new_row_term(mine, other, before, beta, row_term, alpha):
    count = before.shape[0]
    norm = jnp.sqrt(unpack(mine[count].astype(F32)) + unpack(other[count].astype(F32)) + EPS)
    alpha[...] = jnp.broadcast_to(norm, alpha.shape)
    product = mine[:count].astype(F32) + other[:count].astype(F32)
    row_term[...] = product * (1.0 / alpha[...])[None] - before[...] * (alpha[...] / beta[...])[None]


def back_kernel(here, row, spot, mine, other, before, beta, blocks, row_term, alpha, total, sent):
    new_row_term(mine, other, before, beta, row_term, alpha)
    send_sums(here, row, spot, row_term, blocks, total, sent)


def diagonal(count):
    lanes = (count, 128)
    return lax.broadcasted_iota(jnp.int32, lanes, 0) == lax.broadcasted_iota(jnp.int32, lanes, 1)


def finish_kernel(mine, other, before, beta, after, row_term, alpha, norms):
    new_row_term(mine, other, before, beta, row_term, alpha)
    total = squares(row_term[...])
    flat = jnp.sum(jnp.where(diagonal(total.shape[0]), total, 0.0), axis=0, keepdims=True)
    norms[...] = jnp.broadcast_to(flat[None], norms.shape)


def forward_kernel(step, row, spot, mine, other, stored, product, total):
    half = mine.shape[0]
    total[...] = jnp.zeros_like(total)

    def pick(n):
        at = spot[n]
        near = mine[jnp.minimum(at, half - 1)].astype(F32)
        far = other[jnp.maximum(at - half, 0)].astype(F32)
        return jnp.where(at < half, near, far)

    accumulate(block_pair, pick, lambda n: row[n], lambda n: stored[pl.ds(n, 2)], total, 0, row.shape[0])
    count = total.shape[0]
    product[:count] = total[...].astype(BF16)
    norm = jnp.zeros(total.shape[1:], F32)
    for last in range(step - 1, half, step):
        norm = norm + mine[last].astype(F32) + other[last].astype(F32)
    product[count] = pack(unpack(norm), 0)


def advance(state, alpha, beta):
    col_term, search, iterate, rhobar, phibar = state
    fresh = col_term / alpha
    rotation = jnp.sqrt(rhobar * rhobar + beta * beta)
    cosine = rhobar / rotation
    sine = beta / rotation
    theta = sine * alpha
    phi = cosine * phibar
    iterate = iterate + (phi / rotation) * search
    search = fresh - (theta / rotation) * search
    return fresh, search, iterate, -cosine * alpha, sine * phibar


def times(field, high, low, side):
    top = field.astype(BF16)
    rest = (field - top.astype(F32)).astype(BF16)
    dims = (((1,), (side,)), ((), ()))
    both = lax.dot_general(jnp.concatenate([top, rest], axis=0), high, dims, preferred_element_type=F32)
    half = field.shape[0]
    return both[:half] + both[half:] + lax.dot_general(top, low, dims, preferred_element_type=F32)


def column_kernel(sweep, chunks, *refs):
    if sweep == 0:
        precond, col_term, beta, scaled, high, low = refs
        top = precond[...].astype(BF16)
        high[...] = top
        low[...] = (precond[...] - top.astype(F32)).astype(BF16)
    elif sweep == 1:
        high, low, before, alpha, beta_before, col_term, beta, scaled, search, iterate, rhobar, phibar = refs
        fresh = before[...] / alpha[...][None]
        search[...] = fresh
        iterate[...] = jnp.zeros_like(iterate)
        rhobar[...] = alpha[...]
        phibar[...] = beta_before[...]
    else:
        (high, low, before, alpha, beta_before, search_in, iterate_in, rhobar_in, phibar_in) = refs[:9]
        col_term, beta, scaled, search, iterate, rhobar, phibar = refs[9:]
        state = (before[...], search_in[...], iterate_in[...], rhobar_in[...], phibar_in[...])
        fresh, search[...], iterate[...], rhobar[...], phibar[...] = advance(state, alpha[...], beta_before[...])
    own = col_term.shape[0]
    gathered = jnp.sum(chunks[...].astype(F32), axis=0)
    beta[...] = jnp.broadcast_to(jnp.sqrt(unpack(gathered[own]) + EPS), beta.shape)
    gathered = gathered * (1.0 / beta[...])[None]
    terms = [times(gathered[c], high[c], low[c], 1) for c in range(own)]
    if sweep > 0:
        terms = [terms[c] - beta[...] * fresh[c] for c in range(own)]
    norm = sum(term * term for term in terms)
    wholes = [times(terms[c], high[c], low[c], 0).astype(BF16) for c in range(own)]
    for c in range(own):
        col_term[c] = terms[c]
        scaled[:, c] = jnp.broadcast_to(wholes[c][None], (scaled.shape[0],) + wholes[c].shape)
    packed = pack(jnp.sum(norm, axis=-1, keepdims=True), 0)
    scaled[:, own] = jnp.broadcast_to(packed[None], (scaled.shape[0],) + packed.shape)


def prepare_kernel(after, high, low, *refs):
    half = len(refs) // 2
    for field, out in zip(refs[:half], refs[half:]):
        for c in range(field.shape[0]):
            out[c] = times(field[c], high[c], low[c], 0)


def last_kernel(norms, row_term, before, search, iterate, alpha, beta_before, rhobar, phibar, out, left):
    flat = jnp.sum(norms[...], axis=0)
    total = jnp.sum(jnp.where(diagonal(alpha.shape[0]), flat, 0.0), axis=-1, keepdims=True)
    beta = jnp.broadcast_to(jnp.sqrt(total + EPS), alpha.shape)
    left[...] = row_term[...] * (1.0 / beta)[None]
    state = (before[...], search[...], iterate[...], rhobar[...], phibar[...])
    _, direction, solved, rho, phi = advance(state, alpha[...], beta_before[...])
    rotation = jnp.sqrt(rho * rho + beta * beta)
    out[...] = solved + ((rho / rotation) * phi / rotation) * direction


def call(kernel, out_shape, operands, scalars=0, scratch=(), name=None, space=pltpu.VMEM, room=8, cost=None):
    return pl.pallas_call(
        kernel,
        out_shape=out_shape,
        in_specs=[SM] * scalars + [pl.BlockSpec(memory_space=space)] * (len(operands) - scalars),
        out_specs=jax.tree.map(lambda _: VM, out_shape),
        scratch_shapes=list(scratch),
        compiler_params=pltpu.CompilerParams(vmem_limit_bytes=room << 20),
        cost_estimate=cost,
        name=name,
    )(*operands)


def shards(blocks, block_row, block_col, right_sides, precond):
    rows, rhs, size = right_sides.shape
    own = precond.shape[0]
    devices = lax.axis_size("rows")
    chips = devices // 2
    half = chips * (own + 1)
    core = lax.rem(lax.axis_index("rows"), 2)
    here = core[None].astype(jnp.int32)
    spot = call(
        functools.partial(place_kernel, own, half), like(block_col.shape, jnp.int32), (here, block_col), 1, name="place"
    )
    same_core = [[2 * chip + c for chip in range(chips)] for c in range(2)]
    swap = [(d, d ^ 1) for d in range(devices)]

    def exchange(parts):
        return lax.all_to_all(parts, "rows", 0, 0, axis_index_groups=same_core, tiled=True)

    def core_swap(array):
        return lax.ppermute(array, "rows", swap)

    part = like((chips, own + 1, rhs, size), BF16)
    norm = like((rhs, size))
    field = like((own, rhs, size))
    row_field = like((rows, rhs, size))
    sums = like((2 * half, rhs, size))

    def scatter(total, sent):
        return exchange(call(add_kernel, part, (total, core_swap(sent)), name="add_cores"))

    in_hbm = [pltpu.with_memory_space_constraint(a, pltpu.HBM) for a in (block_row, block_col, right_sides, blocks)]
    count = blocks.shape[0]
    plain = count * PLAIN[0] // PLAIN[1] // 2 * 2
    total, sent, stored = call(
        functools.partial(first_kernel, own),
        [sums, part, pltpu.VMEM((count + plain,) + blocks.shape[1:], BF16)],
        (here, *in_hbm),
        1,
        [
            pltpu.VMEM((count - plain,) + blocks.shape[1:], BF16),
            pltpu.VMEM((rows, rhs, size), F32),
            pltpu.SMEM(block_row.shape, jnp.int32),
            pltpu.SMEM(block_col.shape, jnp.int32),
            pltpu.SemaphoreType.DMA((count // part_of(count, plain) + 3,)),
        ],
        "first_backward",
        pl.ANY,
        7 + (2 * (count - plain) * size * size >> 20),
    )
    stored = pltpu.with_memory_space_constraint(stored, pltpu.VMEM)
    row_term = right_sides
    col_term = alpha = beta = None
    state = []
    for sweep in range(ITERS + 1):
        chunks = scatter(total, sent)
        carried = [precond] if sweep == 0 else [high, low, col_term, alpha, beta] + state
        new = call(
            functools.partial(column_kernel, sweep),
            [field, norm, part] + ([like(precond.shape, BF16)] * 2 if sweep == 0 else [field, field, norm, norm]),
            (chunks, *carried),
            name=f"columns_{sweep}",
        )
        col_term, beta, scaled = new[:3]
        if sweep == ITERS:
            break
        if sweep == 0:
            high, low = new[3:]
        else:
            state = list(new[3:])
        mine = exchange(scaled)
        other = core_swap(mine)
        flat = (half, rhs, size)
        product = call(
            functools.partial(forward_kernel, own + 1),
            like((rows + 1, rhs, size), BF16),
            (block_row, spot, mine.reshape(flat), other.reshape(flat), stored),
            2,
            [pltpu.VMEM((rows, rhs, size), F32)],
            f"forward_{sweep}",
        )
        crossed = lax.ppermute(product, "cols", [(0, 1), (1, 0)])
        loaded = call(
            load_kernel,
            pltpu.VMEM(blocks.shape, BF16),
            (in_hbm[3], product),
            0,
            [pltpu.SemaphoreType.DMA((unroll_of(count, 8),))],
            f"load_{sweep}",
            pl.ANY,
            1,
            pl.CostEstimate(flops=0, bytes_accessed=4 * count * size * size, transcendentals=0),
        )
        loaded = pltpu.with_memory_space_constraint(loaded, pltpu.VMEM)
        if sweep < ITERS - 1:
            row_term, alpha, total, sent = call(
                back_kernel,
                [row_field, norm, sums, part],
                (here, block_row, spot, product, crossed, row_term, beta, loaded),
                3,
                (),
                f"backward_{sweep}",
            )
        else:
            search, iterate, rhobar, phibar = state
            fields = (col_term, search, iterate)
            ready = call(prepare_kernel, [field] * 3, (product, high, low, *fields), name="prepare")
            row_term, alpha, norms = call(
                finish_kernel,
                [row_field, norm, like((devices, 1, size))],
                (product, crossed, row_term, beta, ready[0]),
                name="finish_rows",
            )
            factors = (alpha, beta, rhobar, phibar)
            total, sent = call(
                dead_kernel, [sums, part], (here, block_row, spot, row_term, loaded), 3, (), "last_backward"
            )
    norms = lax.all_to_all(norms, "rows", 0, 0, tiled=True)
    return call(last_kernel, [field, row_field], (norms, row_term, *ready, *factors), name="last")


def solution(mesh):
    return jax.shard_map(
        shards,
        mesh=mesh,
        in_specs=(
            P(("rows", "cols"), None, None),
            P(("rows", "cols")),
            P(("rows", "cols")),
            P("rows", None, None),
            P(("cols", "rows"), None, None),
        ),
        out_specs=(P(("cols", "rows"), None, None), P("rows", None, None)),
        check_vma=False,
    )
```

```python
import functools

import jax
import jax.numpy as jnp
from jax import lax
from jax.experimental import pallas as pl
from jax.experimental.pallas import tpu as pltpu
from jax.sharding import PartitionSpec as P

ITERS = 3


EPS = 1e-06
F32 = jnp.float32
BF16 = jnp.bfloat16
VM = pl.BlockSpec(memory_space=pltpu.VMEM)
SM = pl.BlockSpec(memory_space=pltpu.SMEM)
LATE = 16
AHEAD = 5
PLAIN = (0, 1)


def like(shape, dtype=F32):
    return jax.ShapeDtypeStruct(shape, dtype)


def pack(total, first):
    half = total * 0.5
    top = half.astype(BF16).astype(F32)
    middle = (half - top).astype(BF16).astype(F32)
    low = half - top - middle
    lane = lax.broadcasted_iota(jnp.int32, (total.shape[0], 128), 1) - first
    terms = jnp.where(lane == 0, top, jnp.where(lane == 1, middle, jnp.where(lane == 2, low, 0.0)))
    return terms.astype(BF16)


def unpack(block):
    return jnp.sum(block, axis=-1, keepdims=True) * 2.0


def squares(field):
    return jnp.sum(jnp.sum(field * field, axis=0), axis=-1, keepdims=True)


def part_of(whole, plain):
    return next(u for u in (64, 32, 16, 8, 4, 2) if whole % u == 0 and plain % u == 0)


def unroll_of(count, most):
    return next(u for u in (640, 320, 160, 128, 64, 32, 16, 8, 4, 2) if u <= most and count % u == 0)


def accumulate(products, pick, target, get, total, first, count, most=640, arrive=None, also=None):
    if count == 0:
        return
    unroll = unroll_of(count, most)

    def add(base, pending):
        at, term = pending
        spot = target(base + at)
        total[spot] = total[spot] + term

    def step(i, carry):
        base = first + i * unroll
        if arrive is not None:
            arrive(first // unroll + i)
        pending = []
        for u in range(0, unroll, 2):
            pair = jnp.concatenate([pick(base + u), pick(base + u + 1)], axis=0)
            if also is not None:
                also(base + u)
                also(base + u + 1)
            pending += list(zip((u, u + 1), products(pair, get(base + u))))
            while len(pending) > LATE:
                add(base, pending.pop(0))
        for item in pending:
            add(base, item)
        return carry

    lax.fori_loop(0, count // unroll, step, 0)


def block_pair(pair, blocks):
    half = pair.shape[0] // 2
    none = jnp.zeros((half, pair.shape[1]), F32)
    spread = jnp.concatenate(
        [jnp.concatenate([pair[:half], none], axis=1), jnp.concatenate([none, pair[half:]], axis=1)], axis=0
    )
    both = jnp.dot(spread.astype(BF16), blocks.reshape(-1, blocks.shape[2]), preferred_element_type=F32)
    return both[:half], both[half:]


def finish_sums(here, row_term, sent, total):
    half = sent.shape[0] * sent.shape[1]
    sent[...] = total[half:].astype(BF16).reshape(sent.shape)
    norm = pack(squares(row_term[...]), 3 * here[0])
    step = sent.shape[1]
    for chip in range(sent.shape[0]):
        total[chip * step + step - 1] = norm.astype(F32)
        sent[chip, step - 1] = norm


def send_sums(here, row, spot, row_term, blocks, total, sent):
    total[...] = jnp.zeros_like(total)
    get = lambda n: blocks[pl.ds(n, 2)]
    accumulate(block_pair, lambda n: row_term[row[n]], lambda n: spot[n], get, total, 0, row.shape[0])
    finish_sums(here, row_term, sent, total)


def load_kernel(blocks, after, loaded, done):
    parts = done.shape[0]
    count = blocks.shape[0] // parts
    copies = [
        pltpu.make_async_copy(blocks.at[pl.ds(i * count, count)], loaded.at[pl.ds(i * count, count)], done.at[i])
        for i in range(parts)
    ]
    for copy in copies:
        copy.start()
    for copy in copies:
        copy.wait()


def place(column, core, own, half):
    owner = column // own
    return ((owner & 1) ^ core) * half + (owner >> 1) * (own + 1) + column % own


def first_kernel(own, here, row_in, column_in, right_sides, blocks, total, sent, stored, rest, table, row, column, done):
    whole = blocks.shape[0]
    plain = stored.shape[0] - whole
    count = part_of(whole, plain)
    half = sent.shape[0] * sent.shape[1]
    core = here[0]
    shift = own.bit_length() - 1

    def load(i, early):
        to = stored.at[pl.ds(whole + i * count, count)] if early else rest.at[pl.ds(i * count - plain, count)]
        return pltpu.make_async_copy(blocks.at[pl.ds(i * count, count)], to, done.at[i])

    def start(i):
        @pl.when(i < plain // count)
        def _():
            load(i, True).start()

        @pl.when((i >= plain // count) & (i < whole // count))
        def _():
            load(i, False).start()

    small = [
        pltpu.make_async_copy(a, b, done.at[whole // count + i])
        for i, (a, b) in enumerate(((row_in, row), (column_in, column), (right_sides, table)))
    ]
    for copy in small:
        copy.start()
    for i in range(AHEAD):
        start(i)

    def spot(n):
        if own != 1 << shift:
            return place(column[n], core, own, half)
        owner = lax.shift_right_logical(column[n], shift)
        chip = lax.shift_right_logical(owner, 1)
        return ((owner & 1) ^ core) * half + chip * (own + 1) + (column[n] & (own - 1))

    for copy in small:
        copy.wait()
    total[...] = jnp.zeros_like(total)
    for early, first, until in ((True, 0, plain), (False, plain, whole)):
        ref, shifted = (stored, whole) if early else (rest, -plain)

        def arrive(i, early=early):
            load(i, early).wait()
            start(i + AHEAD)

        def turn(n, ref=ref, shifted=shifted):
            stored[n] = ref[shifted + n].T

        def get(n, ref=ref, shifted=shifted):
            return ref[pl.ds(shifted + n, 2)]

        accumulate(
            block_pair, lambda n: table[row[n]], spot, get, total, first, until - first, count, arrive, turn
        )
    finish_sums(here, table, sent, total)


def place_kernel(own, half, here, column, spot):
    spot[...] = place(column[...], here[0], own, half)


def add_kernel(total, arrived, both):
    half = both.shape[0] * both.shape[1]
    both[...] = (total[:half].reshape(both.shape) + arrived[...].astype(F32)).astype(BF16)


def dead_kernel(here, row, spot, row_term, blocks, total, sent):
    send_sums(here, row, spot, row_term, blocks, total, sent)


def new_row_term(mine, other, before, beta, row_term, alpha):
    count = before.shape[0]
    norm = jnp.sqrt(unpack(mine[count].astype(F32)) + unpack(other[count].astype(F32)) + EPS)
    alpha[...] = jnp.broadcast_to(norm, alpha.shape)
    product = mine[:count].astype(F32) + other[:count].astype(F32)
    row_term[...] = product * (1.0 / alpha[...])[None] - before[...] * (alpha[...] / beta[...])[None]


def back_kernel(here, row, spot, mine, other, before, beta, blocks, row_term, alpha, total, sent):
    new_row_term(mine, other, before, beta, row_term, alpha)
    send_sums(here, row, spot, row_term, blocks, total, sent)


def diagonal(count):
    lanes = (count, 128)
    return lax.broadcasted_iota(jnp.int32, lanes, 0) == lax.broadcasted_iota(jnp.int32, lanes, 1)


def finish_kernel(mine, other, before, beta, after, row_term, alpha, norms):
    new_row_term(mine, other, before, beta, row_term, alpha)
    total = squares(row_term[...])
    flat = jnp.sum(jnp.where(diagonal(total.shape[0]), total, 0.0), axis=0, keepdims=True)
    norms[...] = jnp.broadcast_to(flat[None], norms.shape)


def forward_kernel(step, row, spot, mine, other, stored, product, total):
    half = mine.shape[0]
    total[...] = jnp.zeros_like(total)

    def pick(n):
        at = spot[n]
        near = mine[jnp.minimum(at, half - 1)].astype(F32)
        far = other[jnp.maximum(at - half, 0)].astype(F32)
        return jnp.where(at < half, near, far)

    accumulate(block_pair, pick, lambda n: row[n], lambda n: stored[pl.ds(n, 2)], total, 0, row.shape[0])
    count = total.shape[0]
    product[:count] = total[...].astype(BF16)
    norm = jnp.zeros(total.shape[1:], F32)
    for last in range(step - 1, half, step):
        norm = norm + mine[last].astype(F32) + other[last].astype(F32)
    product[count] = pack(unpack(norm), 0)


def advance(state, alpha, beta):
    col_term, search, iterate, rhobar, phibar = state
    fresh = col_term / alpha
    rotation = jnp.sqrt(rhobar * rhobar + beta * beta)
    cosine = rhobar / rotation
    sine = beta / rotation
    theta = sine * alpha
    phi = cosine * phibar
    iterate = iterate + (phi / rotation) * search
    search = fresh - (theta / rotation) * search
    return fresh, search, iterate, -cosine * alpha, sine * phibar


def times(field, high, low, side):
    top = field.astype(BF16)
    rest = (field - top.astype(F32)).astype(BF16)
    dims = (((1,), (side,)), ((), ()))
    both = lax.dot_general(jnp.concatenate([top, rest], axis=0), high, dims, preferred_element_type=F32)
    half = field.shape[0]
    return both[:half] + both[half:] + lax.dot_general(top, low, dims, preferred_element_type=F32)


def column_kernel(sweep, chunks, *refs):
    if sweep == 0:
        precond, col_term, beta, scaled, high, low = refs
        top = precond[...].astype(BF16)
        high[...] = top
        low[...] = (precond[...] - top.astype(F32)).astype(BF16)
    elif sweep == 1:
        high, low, before, alpha, beta_before, col_term, beta, scaled, search, iterate, rhobar, phibar = refs
        fresh = before[...] / alpha[...][None]
        search[...] = fresh
        iterate[...] = jnp.zeros_like(iterate)
        rhobar[...] = alpha[...]
        phibar[...] = beta_before[...]
    else:
        (high, low, before, alpha, beta_before, search_in, iterate_in, rhobar_in, phibar_in) = refs[:9]
        col_term, beta, scaled, search, iterate, rhobar, phibar = refs[9:]
        state = (before[...], search_in[...], iterate_in[...], rhobar_in[...], phibar_in[...])
        fresh, search[...], iterate[...], rhobar[...], phibar[...] = advance(state, alpha[...], beta_before[...])
    own = col_term.shape[0]
    gathered = jnp.sum(chunks[...].astype(F32), axis=0)
    beta[...] = jnp.broadcast_to(jnp.sqrt(unpack(gathered[own]) + EPS), beta.shape)
    gathered = gathered * (1.0 / beta[...])[None]
    terms = [times(gathered[c], high[c], low[c], 1) for c in range(own)]
    if sweep > 0:
        terms = [terms[c] - beta[...] * fresh[c] for c in range(own)]
    norm = sum(term * term for term in terms)
    wholes = [times(terms[c], high[c], low[c], 0).astype(BF16) for c in range(own)]
    for c in range(own):
        col_term[c] = terms[c]
        scaled[:, c] = jnp.broadcast_to(wholes[c][None], (scaled.shape[0],) + wholes[c].shape)
    packed = pack(jnp.sum(norm, axis=-1, keepdims=True), 0)
    scaled[:, own] = jnp.broadcast_to(packed[None], (scaled.shape[0],) + packed.shape)


def prepare_kernel(after, high, low, *refs):
    half = len(refs) // 2
    for field, out in zip(refs[:half], refs[half:]):
        for c in range(field.shape[0]):
            out[c] = times(field[c], high[c], low[c], 0)


def last_kernel(norms, row_term, before, search, iterate, alpha, beta_before, rhobar, phibar, out, left):
    flat = jnp.sum(norms[...], axis=0)
    total = jnp.sum(jnp.where(diagonal(alpha.shape[0]), flat, 0.0), axis=-1, keepdims=True)
    beta = jnp.broadcast_to(jnp.sqrt(total + EPS), alpha.shape)
    left[...] = row_term[...] * (1.0 / beta)[None]
    state = (before[...], search[...], iterate[...], rhobar[...], phibar[...])
    _, direction, solved, rho, phi = advance(state, alpha[...], beta_before[...])
    rotation = jnp.sqrt(rho * rho + beta * beta)
    out[...] = solved + ((rho / rotation) * phi / rotation) * direction


def call(kernel, out_shape, operands, scalars=0, scratch=(), name=None, space=pltpu.VMEM, room=8, cost=None):
    return pl.pallas_call(
        kernel,
        out_shape=out_shape,
        in_specs=[SM] * scalars + [pl.BlockSpec(memory_space=space)] * (len(operands) - scalars),
        out_specs=jax.tree.map(lambda _: VM, out_shape),
        scratch_shapes=list(scratch),
        compiler_params=pltpu.CompilerParams(vmem_limit_bytes=room << 20),
        cost_estimate=cost,
        name=name,
    )(*operands)


def shards(blocks, block_row, block_col, right_sides, precond):
    rows, rhs, size = right_sides.shape
    own = precond.shape[0]
    devices = lax.axis_size("rows")
    chips = devices // 2
    half = chips * (own + 1)
    core = lax.rem(lax.axis_index("rows"), 2)
    here = core[None].astype(jnp.int32)
    spot = call(
        functools.partial(place_kernel, own, half), like(block_col.shape, jnp.int32), (here, block_col), 1, name="place"
    )
    same_core = [[2 * chip + c for chip in range(chips)] for c in range(2)]
    swap = [(d, d ^ 1) for d in range(devices)]

    def exchange(parts):
        return lax.all_to_all(parts, "rows", 0, 0, axis_index_groups=same_core, tiled=True)

    def core_swap(array):
        return lax.ppermute(array, "rows", swap)

    part = like((chips, own + 1, rhs, size), BF16)
    norm = like((rhs, size))
    field = like((own, rhs, size))
    row_field = like((rows, rhs, size))
    sums = like((2 * half, rhs, size))

    def scatter(total, sent):
        return exchange(call(add_kernel, part, (total, core_swap(sent)), name="add_cores"))

    in_hbm = [pltpu.with_memory_space_constraint(a, pltpu.HBM) for a in (block_row, block_col, right_sides, blocks)]
    count = blocks.shape[0]
    plain = count * PLAIN[0] // PLAIN[1] // 2 * 2
    total, sent, stored = call(
        functools.partial(first_kernel, own),
        [sums, part, pltpu.VMEM((count + plain,) + blocks.shape[1:], BF16)],
        (here, *in_hbm),
        1,
        [
            pltpu.VMEM((count - plain,) + blocks.shape[1:], BF16),
            pltpu.VMEM((rows, rhs, size), F32),
            pltpu.SMEM(block_row.shape, jnp.int32),
            pltpu.SMEM(block_col.shape, jnp.int32),
            pltpu.SemaphoreType.DMA((count // part_of(count, plain) + 3,)),
        ],
        "first_backward",
        pl.ANY,
        7 + (2 * (count - plain) * size * size >> 20),
    )
    stored = pltpu.with_memory_space_constraint(stored, pltpu.VMEM)
    row_term = right_sides
    col_term = alpha = beta = None
    state = []
    for sweep in range(ITERS + 1):
        chunks = scatter(total, sent)
        carried = [precond] if sweep == 0 else [high, low, col_term, alpha, beta] + state
        new = call(
            functools.partial(column_kernel, sweep),
            [field, norm, part] + ([like(precond.shape, BF16)] * 2 if sweep == 0 else [field, field, norm, norm]),
            (chunks, *carried),
            name=f"columns_{sweep}",
        )
        col_term, beta, scaled = new[:3]
        if sweep == ITERS:
            break
        if sweep == 0:
            high, low = new[3:]
        else:
            state = list(new[3:])
        mine = exchange(scaled)
        other = core_swap(mine)
        flat = (half, rhs, size)
        product = call(
            functools.partial(forward_kernel, own + 1),
            like((rows + 1, rhs, size), BF16),
            (block_row, spot, mine.reshape(flat), other.reshape(flat), stored),
            2,
            [pltpu.VMEM((rows, rhs, size), F32)],
            f"forward_{sweep}",
        )
        crossed = lax.ppermute(product, "cols", [(0, 1), (1, 0)])
        loaded = call(
            load_kernel,
            pltpu.VMEM(blocks.shape, BF16),
            (in_hbm[3], product),
            0,
            [pltpu.SemaphoreType.DMA((unroll_of(count, 8),))],
            f"load_{sweep}",
            pl.ANY,
            1,
            pl.CostEstimate(flops=0, bytes_accessed=4 * count * size * size, transcendentals=0),
        )
        loaded = pltpu.with_memory_space_constraint(loaded, pltpu.VMEM)
        if sweep < ITERS - 1:
            row_term, alpha, total, sent = call(
                back_kernel,
                [row_field, norm, sums, part],
                (here, block_row, spot, product, crossed, row_term, beta, loaded),
                3,
                (),
                f"backward_{sweep}",
            )
        else:
            search, iterate, rhobar, phibar = state
            fields = (col_term, search, iterate)
            ready = call(prepare_kernel, [field] * 3, (product, high, low, *fields), name="prepare")
            row_term, alpha, norms = call(
                finish_kernel,
                [row_field, norm, like((devices, 1, size))],
                (product, crossed, row_term, beta, ready[0]),
                name="finish_rows",
            )
            factors = (alpha, beta, rhobar, phibar)
            total, sent = call(
                dead_kernel, [sums, part], (here, block_row, spot, row_term, loaded), 3, (), "last_backward"
            )
    norms = lax.all_to_all(norms, "rows", 0, 0, tiled=True)
    return call(last_kernel, [field, row_field], (norms, row_term, *ready, *factors), name="last")


def solution(mesh):
    return jax.shard_map(
        shards,
        mesh=mesh,
        in_specs=(
            P(("rows", "cols"), None, None),
            P(("rows", "cols")),
            P(("rows", "cols")),
            P("rows", None, None),
            P(("cols", "rows"), None, None),
        ),
        out_specs=(P(("cols", "rows"), None, None), P("rows", None, None)),
        check_vma=False,
    )
```
